128 devices in a mesh: ty: 8 (over z, core), tx: 16 (over x, y).
Axes of the slice: x: 4, y: 4, z: 4, core: 2. Of those that a mesh axis runs over, the one named last changes fastest.
Arguments:
- final_cotangent: float32 [90, 4, 128, 2048], P(None, None, 'ty', 'tx'), may hold values from -6 to 6
- vertical_mixing: float32 [90, 128, 2048], P(None, 'ty', 'tx'), may hold values from 0.05 to 6000
- biharmonic_coef: float32 [90, 4], replicated, may hold values from 0.004 to 0.028
- wet_mask: int32 [128, 2048], P('ty', 'tx'), may hold values from 0 to 1, as said below
- owner_tile: int32 [128, 2048], P('ty', 'tx'), may hold values from 0 to 127, as said below
- control_slot: int32 [128, 2048], P('ty', 'tx'), may hold values from 0 to 15
Outputs:
- initial_cotangent: float32 [90, 4, 128, 2048], P(None, None, 'ty', 'tx')
- control_sensitivity: float32 [4, 2048], P(None, ('ty', 'tx'))
The draws below stay inside these ranges and needn't reach their ends.
Inputs may be any that keep to these rules, and one draw needn't show every extreme that they name: `wet_mask`: 1 marks a wet column; the share of wet columns differs from tile to tile. `owner_tile`: tiles are numbered row-major over the grid of 8 by 16 tiles; the owner's tile row and tile column each differ from those of the column's own tile by at most one, and diagonal neighbours occur.
All inputs are finite; a program needn't handle non-finite values.
Results may differ from the reference program's by a relative error of at most 0.0003.
Values sent between devices are 32-bit elements; how exact they have to be, the bound alone decides.
A program may use at most 128 MiB of HBM per device.

```python
import math
import jax
import jax.numpy as jnp
from jax import lax

LEVEL_TOTAL = 90
CI = 16
CJ = 128
CTRL_DEV = 16
CTRL_TOTAL = 2048
NY = 128
NX = 2048


def owner_layout(key):
    tile_rows = NY // CI
    tile_cols = NX // CJ
    grid_row = jnp.arange(NY)[:, None]
    grid_col = jnp.arange(NX)[None, :]
    band_row = grid_row // CI
    inner_row = grid_row % CI
    band_col = grid_col // CJ
    inner_col = grid_col % CJ
    key_rows, key_cols = jax.random.split(key)
    coin_rows = jax.random.randint(key_rows, (NY, NX), 0, 2)
    coin_cols = jax.random.randint(key_cols, (NY, NX), 0, 2)
    step_row = jnp.where(inner_row < 4, -coin_rows, jnp.where(inner_row >= CI - 4, coin_rows, 0))
    step_col = jnp.where(inner_col < 4, -coin_cols, jnp.where(inner_col >= CJ - 4, coin_cols, 0))
    corner = (inner_row == 0) & (inner_col == 0)
    step_row = jnp.where(corner, -1, step_row)
    step_col = jnp.where(corner, -1, step_col)
    step_row = jnp.where((band_row + step_row < 0) | (band_row + step_row >= tile_rows), 0, step_row)
    step_col = jnp.where((band_col + step_col < 0) | (band_col + step_col >= tile_cols), 0, step_col)
    owners = (band_row + step_row) * tile_cols + (band_col + step_col)
    block_row = jnp.where(step_row == 0, inner_row // 8, jnp.where(step_row < 0, CI // 8 - 1, 0))
    block_col = jnp.where(step_col == 0, inner_col // 16, jnp.where(step_col < 0, CJ // 16 - 1, 0))
    slots = block_row * (CJ // 16) + block_col
    return (owners.astype(jnp.int32), slots.astype(jnp.int32))


def draw_owner_tile(key, part):
    shared = owner_layout(key)
    return shared[0]


def draw_control_slot(key, part):
    shared = owner_layout(key)
    return shared[1]


def draw_wet_mask(key, part):
    key = jax.random.fold_in(key, 3)
    key_tiles, key_cells = jax.random.split(key)
    threshold = jax.random.randint(key_tiles, (NY // CI, NX // CJ), 40, 101)
    threshold = jnp.repeat(jnp.repeat(threshold, CI, axis=0), CJ, axis=1)
    cell_draw = jax.random.randint(key_cells, (NY, NX), 0, 100)
    return (cell_draw < threshold).astype(jnp.int32)


def mixing_field(key, share, strong_low):
    selection_key, intense_key, roughness_key, feeble_key, spike_key, surface_key = jax.random.split(key, 6)
    column_pick = jax.random.randint(selection_key, (NY, NX), 0, 100) < share
    intense_logarithm = jax.random.uniform(intense_key, (NY, NX), jnp.float32, math.log(strong_low), math.log(3000.0))
    roughness_logarithm = jax.random.uniform(roughness_key, (LEVEL_TOTAL, NY, NX), jnp.float32, math.log(0.5), math.log(2.0))
    weak_log = jax.random.uniform(feeble_key, (LEVEL_TOTAL, NY, NX), jnp.float32, math.log(0.05), math.log(5.0))
    spike_levels = jax.random.randint(spike_key, (3,), 1, max(LEVEL_TOTAL, 2))
    mixing_spike = jnp.any(jnp.arange(LEVEL_TOTAL)[:, None] == spike_levels[None, :], axis=1)
    spike_logarithm = jnp.where(mixing_spike, math.log(0.25), 0.0).astype(jnp.float32)
    intense_mixing = intense_logarithm[None] + roughness_logarithm + spike_logarithm[:, None, None]
    field_log = jnp.where(column_pick[None], intense_mixing, weak_log)
    top_log = jax.random.uniform(surface_key, (1, NY, NX), jnp.float32, math.log(0.05), math.log(5.0))
    field_log = jnp.concatenate([top_log, field_log[1:]], axis=0)
    return jnp.exp(field_log).astype(jnp.float32)


def draw_vertical_mixing(key, part):
    key = jax.random.fold_in(key, 4)
    return mixing_field(key, 30, 300.0)


def level_of(key, extent, cuts, smallest, high):
    def one(axis_at, shards_of):
        heights = jax.random.uniform(jax.random.fold_in(jax.random.fold_in(key, 6), axis_at), (shards_of,), jnp.float32, smallest / len(cuts), high / len(cuts))
        return jnp.repeat(jnp.exp(heights), extent[axis_at] // shards_of).reshape((-1,) + (1,) * (len(extent) - axis_at - 1))

    level = one(*cuts[0])
    for cut in cuts[1:]:
        level = level * one(*cut)
    return level


def normal_values(rng, extent, deviation, limit, cuts=(), kind=jnp.bfloat16):
    values = jax.random.normal(rng, extent, jnp.float32) * deviation
    if len(cuts) > 0:
        values = level_of(rng, extent, cuts, -0.22, 0.18) * values
    return jnp.clip(values, min=-limit, max=limit).astype(kind)


def setup_inputs(seed: int = 0) -> dict:
    keys = jax.random.split(jax.random.key(seed), 7)
    final_cotangent = normal_values(keys[0], (LEVEL_TOTAL, 4, NY, NX), 1.0, 6.0, ((2, 8), (3, 16)), jnp.float32)
    vertical_mixing = draw_vertical_mixing(jax.random.fold_in(keys[6], 71), 0)
    biharmonic_coef = jnp.clip(jnp.exp(jax.random.uniform(keys[2], (LEVEL_TOTAL, 4), jnp.float32, math.log(0.004), math.log(0.028))), 0.004, 0.028)
    wet_mask = draw_wet_mask(jax.random.fold_in(keys[6], 71), 0)
    owner_tile = draw_owner_tile(jax.random.fold_in(keys[6], 71), 0)
    control_slot = draw_control_slot(jax.random.fold_in(keys[6], 71), 0)
    return dict(final_cotangent=final_cotangent, vertical_mixing=vertical_mixing, biharmonic_coef=biharmonic_coef, wet_mask=wet_mask, owner_tile=owner_tile, control_slot=control_slot)


THERMAL = 0.6
HALINE = 0.8
CORIOLIS = 0.3
FLUX_SCALE = 0.0625


def factor(mixing):
    zero_level = jnp.zeros_like(mixing[:1])
    upper = jnp.concatenate([mixing[1:], zero_level], axis=0)
    lower = jnp.concatenate([zero_level, mixing[1:]], axis=0)
    surface = jnp.concatenate([mixing[:1], jnp.zeros_like(mixing[1:])], axis=0)
    diagonal = 1.0 + upper + lower + surface

    def eliminate(previous, level_items):
        level_diag, level_low = level_items
        ratio = -level_low / previous
        pivot = level_diag + ratio * level_low
        return pivot, (ratio, 1.0 / pivot)

    top_pivot = diagonal[0]
    _, (ratios, inverses) = lax.scan(eliminate, top_pivot, (diagonal[1:], lower[1:]))
    ratios = jnp.concatenate([jnp.zeros_like(top_pivot)[None], ratios], axis=0)
    inverses = jnp.concatenate([(1.0 / top_pivot)[None], inverses], axis=0)
    return ratios, inverses, upper


def solve(values, ratios, inverses, upper):
    def downward(previous, level_items):
        level_value, level_ratio = level_items
        current = level_value - level_ratio * previous
        return current, current

    _, forward = lax.scan(downward, jnp.zeros_like(values[0]), (values, ratios[:, None]))

    def upward(later_value, level_items):
        level_value, coupling, scaling = level_items
        current = (level_value + coupling * later_value) * scaling
        return current, current

    _, result = lax.scan(upward, jnp.zeros_like(values[0]),
                         (forward, upper[:, None], inverses[:, None]), reverse=True)
    return result


def laplace(values, center_wet, wet_count):
    beside_all = values[..., :-2, 1:-1] + values[..., 2:, 1:-1] + values[..., 1:-1, :-2] + values[..., 1:-1, 2:]
    return center_wet * beside_all - wet_count * values[..., 1:-1, 1:-1]


def horizontal(solved, wet_cells, smoothing):
    wet_count = wet_cells[:-2, 1:-1] + wet_cells[2:, 1:-1] + wet_cells[1:-1, :-2] + wet_cells[1:-1, 2:]
    center_wet = wet_cells[1:-1, 1:-1]
    first = laplace(solved, center_wet, wet_count)
    second = laplace(first, center_wet[1:-1, 1:-1], wet_count[1:-1, 1:-1])
    core = solved[..., 2:-2, 2:-2]
    smooth = core - smoothing * second
    east = solved[..., 2, 2:-2, 3:-1] - solved[..., 2, 2:-2, 1:-3]
    north = solved[..., 3, 3:-1, 2:-2] - solved[..., 3, 1:-3, 2:-2]
    buoyancy = -0.25 * (east + north)
    return jnp.stack([smooth[..., 0, :, :] + THERMAL * buoyancy,
                      smooth[..., 1, :, :] - HALINE * buoyancy,
                      smooth[..., 2, :, :] - CORIOLIS * core[..., 3, :, :],
                      smooth[..., 3, :, :] + CORIOLIS * core[..., 2, :, :]], axis=-3)


def reference(final_cotangent, vertical_mixing, biharmonic_coef, wet_mask, owner_tile, control_slot):
    wet_cells = wet_mask.astype(jnp.float32)
    wet_padded = jnp.pad(wet_cells, ((2, 2), (2, 2)))
    ratios, inverses, upper = factor(vertical_mixing)

    def one_level(level_items):
        level_values, level_gains = level_items
        padded = jnp.pad(level_values, ((0, 0), (2, 2), (2, 2)))
        return horizontal(padded, wet_padded, level_gains[:, None, None])

    adjoint = final_cotangent
    surface_sum = jnp.zeros(final_cotangent.shape[1:], jnp.float32)
    for adjoint_step in range(2):
        masked = adjoint * wet_cells
        surface_sum = surface_sum + masked[0]
        solved = solve(masked, ratios, inverses, upper)
        adjoint = lax.map(one_level, (solved, biharmonic_coef))
    flat_sums = surface_sum.reshape(4, -1)
    targets = (owner_tile * CTRL_DEV + control_slot).reshape(-1).astype(jnp.int32)
    totals = jax.ops.segment_sum(flat_sums.T, targets, num_segments=CTRL_TOTAL).T
    return adjoint, totals * FLUX_SCALE
```

```python
import jax
import jax.numpy as jnp
from jax import lax
from jax.experimental import pallas as pl
from jax.experimental.pallas import tpu as pltpu
from jax.sharding import PartitionSpec as P

LEVELS = 90
CHUNKS = 3
CHUNK = LEVELS // CHUNKS
SLOTS = 16
THERMAL = 0.6
HALINE = 0.8
CORIOLIS = 0.3
FLUX_SCALE = 0.0625
MESH = pl.DeviceIdType.MESH
UP, DOWN, RIGHT, LEFT = (-1, 0), (1, 0), (0, 1), (0, -1)
DOWN_RIGHT, DOWN_LEFT, UP_RIGHT, UP_LEFT = (1, 1), (1, -1), (-1, 1), (-1, -1)
WAYS = (UP, DOWN, RIGHT, LEFT, DOWN_RIGHT, DOWN_LEFT, UP_RIGHT, UP_LEFT)
F32 = jnp.float32


def srl(x, shift):
    return pltpu.roll(x, shift % 8, 0)


def lrl(x, shift):
    return pltpu.roll(x, shift % 128 if isinstance(shift, int) else shift, 1)


def kernel(
    rows_n, cols_n,
    x_hbm, k_hbm, coef, wet_in, owner, slot,
    out_hbm, sens,
    xin, kin, outs, field, gb, invb, ga, inva, dbuf, buoy, wetn, w_own, n_own,
    w_halo, n_halo, w_col, n_col,
    up_send, down_send, col_send, corner_send, up_recv, down_recv, col_recv, corner_recv,
    wrow_send, wcol_send, wcorner_send, wrow_recv, wcol_recv, wcorner_recv,
    upack, dpack, kpack, surf, surf_rows, onehot, ctrl_send, ctrl_recv,
    in_sem, out_sem, send_sem, recv_sem, wsend_sem, wrecv_sem, csend_sem, crecv_sem,
):
    ty = lax.axis_index("ty")
    tx = lax.axis_index("tx")
    sub = lax.broadcasted_iota(jnp.int32, (8, 128), 0)
    lane = lax.broadcasted_iota(jnp.int32, (8, 128), 1)
    even = (sub & 1) == 0
    pair = sub >> 1
    pos = lane & 3
    quad = lane >> 2
    top, bottom = sub == 0, sub == 7
    first, last = lane == 0, lane == 127
    zero = jnp.zeros((8, 128), F32)

    def inside(way):
        row, col = ty + way[0], tx + way[1]
        return (row >= 0) & (row < rows_n) & (col >= 0) & (col < cols_n)

    def back(way):
        return (-way[0], -way[1])

    barrier = pltpu.get_barrier_semaphore()
    count = 0
    for way in WAYS:
        @pl.when(inside(way))
        def _(way=way):
            pl.semaphore_signal(
                barrier, inc=1, device_id=(ty + way[0], tx + way[1]), device_id_type=MESH
            )
        count = count + inside(way).astype(jnp.int32)

    def load(part):
        span = pl.ds(part * CHUNK, CHUNK)
        return (
            pltpu.make_async_copy(k_hbm.at[span], kin.at[span], in_sem.at[0, part]),
            pltpu.make_async_copy(x_hbm.at[span], xin.at[span], in_sem.at[1, part]),
        )

    for part in (2, 1, 0):
        for copy in load(part):
            copy.start()

    for index, way in enumerate(WAYS):
        @pl.when(jnp.logical_not(inside(back(way))))
        def _(index=index, way=way):
            if way in (UP, DOWN):
                target = up_recv if way == UP else down_recv
                def clear(i, _):
                    for phase in range(2):
                        target[phase, i] = zero
                    return 0
                lax.fori_loop(0, LEVELS, clear, 0)
                wrow_recv[index] = zero
            elif way in (RIGHT, LEFT):
                def clear(i, _):
                    for phase in range(2):
                        for c in range(CHUNKS):
                            col_recv[index - 2, phase, c, i] = zero
                    return 0
                lax.fori_loop(0, 8, clear, 0)
                for r in range(2):
                    wcol_recv[index - 2, r] = zero
            else:
                for phase in range(2):
                    for c in range(CHUNKS):
                        corner_recv[index - 4, phase, c] = zero
                wcorner_recv[index - 4] = zero
            ctrl_recv[index] = zero

    def row_pack(x):
        q = []
        for r in range(2):
            acc = srl(x[0][r], 1)
            for v in range(1, 4):
                acc = jnp.where(pair == v, srl(x[v][r], 2 * v + 1), acc)
            q.append(acc)
        return jnp.where(even, srl(q[0], -1), q[1]), jnp.where(even, q[0], srl(q[1], 1))

    def row_around(x0, x1, edge):
        return (
            (jnp.where(top, edge, srl(x1, 1)), x0),
            (x1, jnp.where(bottom, edge, srl(x0, -1))),
        )

    def col_around(x, edge):
        return jnp.where(first, edge, lrl(x, 1)), jnp.where(last, edge, lrl(x, -1))

    def swap(x):
        return jnp.where(pos == 1, lrl(x, -1), lrl(x, 1))

    def corner_of(ul, ur, dl, dr):
        return jnp.where(even, jnp.where(pos < 2, dl, dr), jnp.where(pos < 2, ul, ur))

    def packed_sum(u, own, edge):
        above, below = row_around(u[0], u[1], edge)
        result = []
        for r in range(2):
            e = jnp.where(pos < 2, u[r], own[r])
            f = jnp.where(pos < 2, own[r], u[r])
            beside = jnp.where(pos < 2, lrl(e, 1) + lrl(e, -1), lrl(f, 1) + lrl(f, -1))
            result.append(beside + above[r] + below[r])
        return result

    def halo_rows(up_r, down_r, up_s, down_s):
        line = jnp.where(even, up_r, down_r)
        beyond = jnp.where(even, srl(up_r + down_s, -1), srl(down_r + up_s, 1))
        return line, beyond

    wetn[...] = wet_in[...].astype(F32)
    w = [wetn[pl.ds(r, 8, stride=2), :] for r in range(2)]
    for r in range(2):
        w_own[r] = w[r]

    def tile4(x):
        x = jnp.where(lane < 4, lrl(x, 2), 0.0)
        for step in (4, 8, 16, 32, 64):
            x = x + lrl(x, step)
        return x

    wu, wd = row_pack([w] * 4)
    wrow_send[0] = wu
    wrow_send[1] = wd
    for r in range(2):
        wcol_send[r] = tile4(w[r])
    wcorner_send[...] = tile4(jnp.where(even, wu, wd))

    def eliminate_up(part, carry):
        for copy in load(part):
            copy.wait()

        def body(i, carry):
            e, g, y = carry
            for step in range(5):
                l = part * CHUNK + CHUNK - 1 - (i * 5 + step)
                masked = [
                    [xin[l, v, pl.ds(r, 8, stride=2), :] * w[r] for r in range(2)] for v in range(4)
                ]
                y = tuple(
                    masked[v][r] + g[r] * y[v * 2 + r] for v in range(4) for r in range(2)
                )
                new_e, new_g = [], []
                for r in range(2):
                    k = kin[l, pl.ds(r, 8, stride=2), :]
                    inverse = 1.0 / (e[r] + k)
                    gain = k * inverse
                    invb[l, r] = inverse
                    gb[l, r] = gain
                    new_g.append(gain)
                    new_e.append(1.0 + gain * e[r])
                e, g = tuple(new_e), tuple(new_g)
                for n in range(8):
                    field[l, n] = y[n]
            return e, g, y

        return lax.fori_loop(0, CHUNK // 5, body, carry)

    one = jnp.ones((8, 128), F32)
    carry = ((one, one), (zero, zero), (zero,) * 8)
    for part in (2, 1, 0):
        carry = eliminate_up(part, carry)
    for v in range(4):
        for r in range(2):
            surf[v * 2 + r] = xin[0, v, pl.ds(r, 8, stride=2), :] * w[r]

    def substitute(phase, part, carry, upward):
        gain, inverse = (ga, inva) if upward else (gb, invb)

        def body(i, z):
            for step in range(5):
                n = i * 5 + step
                l = part * CHUNK + (CHUNK - 1 - n if upward else n)
                z = tuple(
                    field[l, n] * inverse[l, n % 2] + gain[l, n % 2] * z[n] for n in range(8)
                )
                for n in range(8):
                    field[l, n] = z[n]
                up, down = row_pack([[z[2 * v], z[2 * v + 1]] for v in range(4)])
                up_send[phase, l] = up
                down_send[phase, l] = down
            return z

        return lax.fori_loop(0, CHUNK // 5, body, carry)

    def pack_columns(phase, part):
        def body(i, acc):
            acc = list(acc)
            for step in range(5):
                j = i * 5 + step
                l = part * CHUNK + j
                here = quad == j
                for n in range(8):
                    acc[n] = jnp.where(here, lrl(field[l, n], 4 * j + 2), acc[n])
                ends = jnp.where(even, up_send[phase, l], down_send[phase, l])
                acc[8] = jnp.where(here, lrl(ends, 4 * j + 2), acc[8])
            return tuple(acc)

        acc = lax.fori_loop(0, CHUNK // 5, body, (zero,) * 9)
        for n in range(8):
            col_send[phase, part, n] = acc[n]
        corner_send[phase, part] = acc[8]

    def message(phase, part, way):
        span = pl.ds(part * CHUNK, CHUNK)
        index = WAYS.index(way)
        if way == UP:
            src, dst = up_send.at[phase, span], up_recv.at[phase, span]
        elif way == DOWN:
            src, dst = down_send.at[phase, span], down_recv.at[phase, span]
        elif way in (RIGHT, LEFT):
            src, dst = col_send.at[phase, part], col_recv.at[index - 2, phase, part]
        else:
            src, dst = corner_send.at[phase, part], corner_recv.at[index - 4, phase, part]
        return pltpu.make_async_remote_copy(
            src_ref=src, dst_ref=dst,
            send_sem=send_sem.at[phase, part, index], recv_sem=recv_sem.at[phase, part, index],
            device_id=(ty + way[0], tx + way[1]), device_id_type=MESH,
        )

    def wet_message(way):
        index = WAYS.index(way)
        if way in (UP, DOWN):
            src, dst = wrow_send.at[index], wrow_recv.at[index]
        elif way in (RIGHT, LEFT):
            src, dst = wcol_send, wcol_recv.at[index - 2]
        else:
            src, dst = wcorner_send, wcorner_recv.at[index - 4]
        return pltpu.make_async_remote_copy(
            src_ref=src, dst_ref=dst, send_sem=wsend_sem.at[index], recv_sem=wrecv_sem.at[index],
            device_id=(ty + way[0], tx + way[1]), device_id_type=MESH,
        )

    def ctrl_message(way):
        index = WAYS.index(way)
        return pltpu.make_async_remote_copy(
            src_ref=ctrl_send.at[index], dst_ref=ctrl_recv.at[index],
            send_sem=csend_sem.at[index], recv_sem=crecv_sem.at[index],
            device_id=(ty + way[0], tx + way[1]), device_id_type=MESH,
        )

    def start(make, ways):
        for way in ways:
            @pl.when(inside(way))
            def _(way=way):
                make(way).start()

    def receive(make, ways):
        for way in ways:
            @pl.when(inside(back(way)))
            def _(way=way):
                make(way).wait_recv()

    def sent(make, ways):
        for way in ways:
            @pl.when(inside(way))
            def _(way=way):
                make(way).wait_send()

    def solve_and_send(phase, upward, ready):
        z = (zero,) * 8
        for part in ((2, 1, 0) if upward else (0, 1, 2)):
            z = substitute(phase, part, z, upward)
            if ready is not None:
                ready()
                ready = None
            start(lambda way: message(phase, part, way), WAYS[:2])
            pack_columns(phase, part)
            start(lambda way: message(phase, part, way), WAYS[2:])

    def enter():
        pl.semaphore_wait(barrier, count)
        start(wet_message, WAYS)

    solve_and_send(0, False, enter)

    kin[LEVELS] = jnp.zeros((16, 128), F32)

    def factor_body(i, e):
        for step in range(5):
            l = i * 5 + step
            new_e = []
            for r in range(2):
                k = kin[l + 1, pl.ds(r, 8, stride=2), :]
                inverse = 1.0 / (e[r] + k)
                gain = k * inverse
                inva[l, r] = inverse
                ga[l, r] = gain
                new_e.append(1.0 + gain * e[r])
            e = tuple(new_e)
        return e

    lax.fori_loop(
        0, LEVELS // 5, factor_body, tuple(1.0 + kin[0, pl.ds(r, 8, stride=2), :] for r in range(2))
    )

    shift = cols_n.bit_length() - 1
    own_row = (owner[...] >> shift) - ty
    own_col = (owner[...] & (cols_n - 1)) - tx
    cell = ((own_row + 1) * 3 + own_col + 1) * SLOTS + slot[...]
    numbers = lax.broadcasted_iota(jnp.int32, (9 * SLOTS, 128), 0)
    for row in range(16):
        hit = numbers == cell[row:row + 1, :]
        onehot[:, row * 128:(row + 1) * 128] = jnp.where(hit, 1.0, 0.0).astype(jnp.bfloat16)

    receive(wet_message, WAYS)
    wk = corner_of(wcorner_recv[0], wcorner_recv[1], wcorner_recv[2], wcorner_recv[3])
    wu2 = [jnp.where(pos < 2, wcol_recv[0, r], wcol_recv[1, r]) for r in range(2)]
    counts = packed_sum(wu2, [wcol_send[r] for r in range(2)], srl(wk, 7))
    for r in range(2):
        w_col[r] = wu2[r]
        n_col[r] = counts[r]
    line, beyond = halo_rows(wrow_recv[0], wrow_recv[1], wrow_send[0], wrow_send[1])
    beside = col_around(line, lrl(swap(wk), 126))
    w_halo[...] = line
    n_halo[...] = beyond + beside[0] + beside[1]
    above, below = row_around(w[0], w[1], srl(line, 7))
    for r in range(2):
        beside = col_around(w[r], lrl(swap(wu2[r]), 126))
        n_own[r] = above[r] + below[r] + beside[0] + beside[1]

    def stencil(phase, part, carry, final):
        receive(lambda way: message(phase, part, way), WAYS)
        corner = corner_of(*[corner_recv[n, phase, part] for n in range(4)])
        kpack[...] = swap(corner)
        for v in range(4):
            edge = srl(corner, 7 - 2 * v)
            u = [
                jnp.where(
                    pos < 2, col_recv[0, phase, part, 2 * v + r], col_recv[1, phase, part, 2 * v + r]
                )
                for r in range(2)
            ]
            total = packed_sum(u, [col_send[phase, part, 2 * v + r] for r in range(2)], edge)
            for r in range(2):
                upack[2 * v + r] = swap(u[r])
                dpack[2 * v + r] = swap(w_col[r] * total[r] - n_col[r] * u[r])

        def first_pass(i, _):
            for step in range(3):
                j = i * 3 + step
                l = part * CHUNK + j
                turn = 126 - 4 * j
                line, beyond = halo_rows(
                    up_recv[phase, l], down_recv[phase, l], up_send[phase, l], down_send[phase, l]
                )
                beside = col_around(line, lrl(kpack[...], turn))
                dbuf[j, 8] = w_halo[...] * (beyond + beside[0] + beside[1]) - n_halo[...] * line
                for v in range(4):
                    z = [field[l, 2 * v + r] for r in range(2)]
                    above, below = row_around(z[0], z[1], srl(line, 7 - 2 * v))
                    for r in range(2):
                        n = 2 * v + r
                        west, east = col_around(z[r], lrl(upack[n], turn))
                        dbuf[j, n] = (
                            w_own[r] * ((above[r] + below[r]) + (west + east)) - n_own[r] * z[r]
                        )
                        if v == 2:
                            buoy[j, r] = east - west
                        if v == 3:
                            buoy[j, r] = buoy[j, r] + (below[r] - above[r])
            return 0

        lax.fori_loop(0, CHUNK // 3, first_pass, 0)

        def second_pass(i, carry):
            for step in range(3):
                m = i * 3 + step
                j = CHUNK - 1 - m if final else m
                l = part * CHUNK + j
                turn = 126 - 4 * j
                z = [[field[l, 2 * v + r] for r in range(2)] for v in range(4)]
                line = dbuf[j, 8]
                new = [None] * 8
                for v in range(4):
                    d = [dbuf[j, 2 * v + r] for r in range(2)]
                    above, below = row_around(d[0], d[1], srl(line, 7 - 2 * v))
                    for r in range(2):
                        n = 2 * v + r
                        west, east = col_around(d[r], lrl(dpack[n], turn))
                        second = ((above[r] + below[r]) + (west + east)) - n_own[r] * d[r]
                        if final:
                            second = second * w_own[r]
                        value = z[v][r] - coef[l, v] * second
                        if v == 0:
                            value = value - (0.25 * THERMAL) * buoy[j, r]
                        elif v == 1:
                            value = value + (0.25 * HALINE) * buoy[j, r]
                        elif v == 2:
                            value = value - CORIOLIS * z[3][r]
                        else:
                            value = value + CORIOLIS * z[2][r]
                        new[n] = value
                if final:
                    for n in range(8):
                        outs[l, n // 2, pl.ds(n % 2, 8, stride=2), :] = new[n]
                else:
                    gain, y = carry
                    masked = [new[n] * w_own[n % 2] for n in range(8)]
                    dbuf[j, 9] = zero
                    y = tuple(masked[n] + gain[n % 2] * y[n] for n in range(8))
                    for n in range(8):
                        field[l, n] = y[n]
                    if part == 0 and step == 0:
                        @pl.when(i == 0)
                        def _():
                            for n in range(8):
                                surf[n] = surf[n] + masked[n]
                    carry = ((ga[l, 0], ga[l, 1]), y)
            return carry

        return lax.fori_loop(0, CHUNK // 3, second_pass, carry)

    carry = ((zero, zero), (zero,) * 8)
    for part in range(CHUNKS):
        carry = stencil(0, part, carry, False)

    solve_and_send(1, True, None)

    for v in range(4):
        for r in range(2):
            surf_rows[v, pl.ds(r, 8, stride=2), :] = surf[v * 2 + r]
    values = jnp.concatenate(
        [jnp.concatenate([surf_rows[:, row, :] for row in range(16)], axis=1)] * 2, axis=0
    )
    high = values.astype(jnp.bfloat16).astype(F32)
    rest = values - high
    middle = rest.astype(jnp.bfloat16).astype(F32)
    low = rest - middle
    pieces = jnp.concatenate([high, middle, low, low], axis=0).astype(jnp.bfloat16)
    sums = lax.dot_general(
        pieces, onehot[...], (((1,), (1,)), ((), ())), preferred_element_type=F32
    )
    sums = (sums[0:8] + sums[8:16] + sums[16:24]) * FLUX_SCALE
    near = sums[:, 0:128]
    for index, way in enumerate(WAYS):
        q = (way[0] + 1) * 3 + way[1] + 1
        if q < 8:
            ctrl_send[index] = lrl(near, -SLOTS * q)
        else:
            ctrl_send[index] = zero
            ctrl_send[index, :, 0:SLOTS] = sums[:, 128:128 + SLOTS]
    start(ctrl_message, WAYS)

    def store(part):
        span = pl.ds(part * CHUNK, CHUNK)
        return pltpu.make_async_copy(outs.at[span], out_hbm.at[span], out_sem.at[part])

    for part in (2, 1, 0):
        stencil(1, part, 0, True)
        store(part).start()

    receive(ctrl_message, WAYS)
    total = lrl(near, -SLOTS * 4)
    for index in range(8):
        total = total + ctrl_recv[index]
    sens[...] = total[0:4, 0:SLOTS]

    sent(wet_message, WAYS)
    sent(ctrl_message, WAYS)
    for phase in range(2):
        for part in range(CHUNKS):
            sent(lambda way: message(phase, part, way), WAYS)
    for part in range(CHUNKS):
        store(part).wait()


def build(rows_n, cols_n):
    any_space = pl.BlockSpec(memory_space=pl.ANY)
    vmem = pl.BlockSpec(memory_space=pltpu.VMEM)
    tile = (8, 128)
    scratch = [
        pltpu.VMEM((LEVELS, 4, 16, 128), F32),
        pltpu.VMEM((LEVELS + 1, 16, 128), F32),
        pltpu.VMEM((LEVELS, 4, 16, 128), F32),
        pltpu.VMEM((LEVELS, 8) + tile, F32),
        pltpu.VMEM((LEVELS, 2) + tile, F32),
        pltpu.VMEM((LEVELS, 2) + tile, F32),
        pltpu.VMEM((LEVELS, 2) + tile, F32),
        pltpu.VMEM((LEVELS, 2) + tile, F32),
        pltpu.VMEM((CHUNK, 10) + tile, F32),
        pltpu.VMEM((CHUNK, 2) + tile, F32),
        pltpu.VMEM((16, 128), F32),
        pltpu.VMEM((2,) + tile, F32),
        pltpu.VMEM((2,) + tile, F32),
        pltpu.VMEM(tile, F32),
        pltpu.VMEM(tile, F32),
        pltpu.VMEM((2,) + tile, F32),
        pltpu.VMEM((2,) + tile, F32),
        pltpu.VMEM((2, LEVELS) + tile, F32),
        pltpu.VMEM((2, LEVELS) + tile, F32),
        pltpu.VMEM((2, CHUNKS, 8) + tile, F32),
        pltpu.VMEM((2, CHUNKS) + tile, F32),
        pltpu.VMEM((2, LEVELS) + tile, F32),
        pltpu.VMEM((2, LEVELS) + tile, F32),
        pltpu.VMEM((2, 2, CHUNKS, 8) + tile, F32),
        pltpu.VMEM((4, 2, CHUNKS) + tile, F32),
        pltpu.VMEM((2,) + tile, F32),
        pltpu.VMEM((2,) + tile, F32),
        pltpu.VMEM(tile, F32),
        pltpu.VMEM((2,) + tile, F32),
        pltpu.VMEM((2, 2) + tile, F32),
        pltpu.VMEM((4,) + tile, F32),
        pltpu.VMEM((8,) + tile, F32),
        pltpu.VMEM((8,) + tile, F32),
        pltpu.VMEM(tile, F32),
        pltpu.VMEM((8,) + tile, F32),
        pltpu.VMEM((4, 16, 128), F32),
        pltpu.VMEM((9 * SLOTS, 16 * 128), jnp.bfloat16),
        pltpu.VMEM((8,) + tile, F32),
        pltpu.VMEM((8,) + tile, F32),
        pltpu.SemaphoreType.DMA((2, CHUNKS)),
        pltpu.SemaphoreType.DMA((CHUNKS,)),
        pltpu.SemaphoreType.DMA((2, CHUNKS, 8)),
        pltpu.SemaphoreType.DMA((2, CHUNKS, 8)),
        pltpu.SemaphoreType.DMA((8,)),
        pltpu.SemaphoreType.DMA((8,)),
        pltpu.SemaphoreType.DMA((8,)),
        pltpu.SemaphoreType.DMA((8,)),
    ]

    def body(*refs):
        kernel(rows_n, cols_n, *refs)

    return pl.pallas_call(
        body,
        out_shape=(
            jax.ShapeDtypeStruct((LEVELS, 4, 16, 128), F32),
            jax.ShapeDtypeStruct((4, SLOTS), F32),
        ),
        in_specs=[
            any_space, any_space, pl.BlockSpec(memory_space=pltpu.SMEM), vmem, vmem, vmem,
        ],
        out_specs=(any_space, vmem),
        scratch_shapes=scratch,
        compiler_params=pltpu.CompilerParams(
            collective_id=0, has_side_effects=True, vmem_limit_bytes=48 << 20
        ),
    )


def solution(mesh):
    def per_device(*args):
        return build(mesh.shape["ty"], mesh.shape["tx"])(*args)

    return jax.shard_map(
        per_device,
        mesh=mesh,
        in_specs=(
            P(None, None, "ty", "tx"),
            P(None, "ty", "tx"),
            P(),
            P("ty", "tx"),
            P("ty", "tx"),
            P("ty", "tx"),
        ),
        out_specs=(P(None, None, "ty", "tx"), P(None, ("ty", "tx"))),
        check_vma=False,
    )
```

```python
import jax
import jax.numpy as jnp
from jax import lax
from jax.experimental import pallas as pl
from jax.experimental.pallas import tpu as pltpu
from jax.sharding import PartitionSpec as P

LEVELS = 90
CHUNKS = 3
CHUNK = LEVELS // CHUNKS
SLOTS = 16
UF, US, UC, UK = 10, 10, 30, 30
THERMAL = 0.6
HALINE = 0.8
CORIOLIS = 0.3
FLUX_SCALE = 0.0625
MESH = pl.DeviceIdType.MESH
UP, DOWN, RIGHT, LEFT = (-1, 0), (1, 0), (0, 1), (0, -1)
DOWN_RIGHT, DOWN_LEFT, UP_RIGHT, UP_LEFT = (1, 1), (1, -1), (-1, 1), (-1, -1)
WAYS = (UP, DOWN, RIGHT, LEFT, DOWN_RIGHT, DOWN_LEFT, UP_RIGHT, UP_LEFT)
F32 = jnp.float32


def srl(x, shift):
    return pltpu.roll(x, shift % 8, 0)


def lrl(x, shift):
    return pltpu.roll(x, shift % 128 if isinstance(shift, int) else shift, 1)


def kernel(
    rows_n, cols_n,
    x_hbm, k_hbm, coef_hbm, wet_hbm, owner_hbm, slot_hbm,
    outs, sens,
    xin, kin, coef, wet_in, owner, slot, field, bulk, gb, invb, ga, inva, buoy, wetn, w_own, n_own,
    w_halo, n_halo, w_col, n_col, n_rim, w_line, n_line, w_next, c_col,
    up_send, down_send, col_send, corner_send, up_recv, down_recv, col_recv, corner_recv,
    wrow_send, wcol_send, wcorner_send, wrow_recv, wcol_recv, wcorner_recv,
    rim, kpack, surf, surf_rows, onehot, ctrl_send, ctrl_recv,
    in_sem, small_sem, send_sem, recv_sem, wsend_sem, wrecv_sem, csend_sem, crecv_sem,
):
    ty = lax.axis_index("ty")
    tx = lax.axis_index("tx")
    sub = lax.broadcasted_iota(jnp.int32, (8, 128), 0)
    lane = lax.broadcasted_iota(jnp.int32, (8, 128), 1)
    even = (sub & 1) == 0
    pair = sub >> 1
    pos = lane & 3
    quad = lane >> 2
    top, bottom = sub == 0, sub == 7
    first, last = lane == 0, lane == 127
    zero = jnp.zeros((8, 128), F32)

    def inside(way):
        row, col = ty + way[0], tx + way[1]
        return (row >= 0) & (row < rows_n) & (col >= 0) & (col < cols_n)

    def back(way):
        return (-way[0], -way[1])

    barrier = pltpu.get_barrier_semaphore()
    count = 0
    for way in WAYS:
        @pl.when(inside(way))
        def _(way=way):
            pl.semaphore_signal(
                barrier, inc=1, device_id=(ty + way[0], tx + way[1]), device_id_type=MESH
            )
        count = count + inside(way).astype(jnp.int32)

    def load(part):
        span = pl.ds(part * CHUNK, CHUNK)
        return (
            pltpu.make_async_copy(k_hbm.at[span], kin.at[span], in_sem.at[0, part]),
            pltpu.make_async_copy(x_hbm.at[span], xin.at[span], in_sem.at[1, part]),
        )

    small = [
        pltpu.make_async_copy(src, dst, small_sem.at[n])
        for n, (src, dst) in enumerate(
            ((wet_hbm, wet_in), (coef_hbm, coef), (owner_hbm, owner), (slot_hbm, slot))
        )
    ]
    small[0].start()
    for part in (2, 1, 0):
        for copy in load(part):
            copy.start()
    for copy in small[1:]:
        copy.start()

    for index, way in enumerate(WAYS):
        @pl.when(jnp.logical_not(inside(back(way))))
        def _(index=index, way=way):
            if way in (UP, DOWN):
                target = up_recv if way == UP else down_recv
                def clear(i, _):
                    for phase in range(2):
                        target[phase, i] = zero
                    return 0
                lax.fori_loop(0, LEVELS, clear, 0)
                wrow_recv[index] = zero
            elif way in (RIGHT, LEFT):
                def clear(i, _):
                    for phase in range(2):
                        for c in range(CHUNKS):
                            col_recv[index - 2, phase, c, i] = zero
                    return 0
                lax.fori_loop(0, 8, clear, 0)
                for r in range(2):
                    wcol_recv[index - 2, r] = zero
            else:
                for phase in range(2):
                    for c in range(CHUNKS):
                        corner_recv[index - 4, phase, c] = zero
                wcorner_recv[index - 4] = zero
            ctrl_recv[index] = zero

    def row_pack(x):
        q = []
        for r in range(2):
            acc = srl(x[0][r], 1)
            for v in range(1, 4):
                acc = jnp.where(pair == v, srl(x[v][r], 2 * v + 1), acc)
            q.append(acc)
        return jnp.where(even, srl(q[0], -1), q[1]), jnp.where(even, q[0], srl(q[1], 1))

    def row_around(x0, x1, edge):
        return (
            (jnp.where(top, edge, srl(x1, 1)), x0),
            (x1, jnp.where(bottom, edge, srl(x0, -1))),
        )

    def col_around(x, edge):
        return jnp.where(first, edge, lrl(x, 1)), jnp.where(last, edge, lrl(x, -1))

    def swap(x):
        return jnp.where(pos == 1, lrl(x, -1), lrl(x, 1))

    def corner_of(ul, ur, dl, dr):
        return jnp.where(even, jnp.where(pos < 2, dl, dr), jnp.where(pos < 2, ul, ur))

    def packed_sum(u, own, edge):
        above, below = row_around(u[0], u[1], edge)
        result = []
        for r in range(2):
            e = jnp.where(pos < 2, u[r], own[r])
            f = jnp.where(pos < 2, own[r], u[r])
            beside = jnp.where(pos < 2, lrl(e, 1) + lrl(e, -1), lrl(f, 1) + lrl(f, -1))
            result.append(beside + above[r] + below[r])
        return result

    def halo_rows(up_r, down_r, up_s, down_s):
        line = jnp.where(even, up_r, down_r)
        beyond = jnp.where(even, srl(up_r + down_s, -1), srl(down_r + up_s, 1))
        return line, beyond

    small[0].wait()
    wetn[...] = wet_in[...].astype(F32)
    w = [wetn[pl.ds(r, 8, stride=2), :] for r in range(2)]
    for r in range(2):
        w_own[r] = w[r]

    def tile4(x):
        x = jnp.where(lane < 4, lrl(x, 2), 0.0)
        for step in (4, 8, 16, 32, 64):
            x = x + lrl(x, step)
        return x

    wu, wd = row_pack([w] * 4)
    wrow_send[0] = wu
    wrow_send[1] = wd
    for r in range(2):
        wcol_send[r] = tile4(w[r])
    wcorner_send[...] = tile4(jnp.where(even, wu, wd))

    def eliminate_up(part, carry):
        for copy in load(part):
            copy.wait()

        def body(i, carry):
            e, g, y = carry
            for step in range(5):
                l = part * CHUNK + CHUNK - 1 - (i * 5 + step)
                masked = [
                    [xin[l, v, pl.ds(r, 8, stride=2), :] * w[r] for r in range(2)] for v in range(4)
                ]
                y = tuple(
                    masked[v][r] + g[r] * y[v * 2 + r] for v in range(4) for r in range(2)
                )
                new_e, new_g = [], []
                for r in range(2):
                    k = kin[l, pl.ds(r, 8, stride=2), :]
                    inverse = 1.0 / (e[r] + k)
                    gain = k * inverse
                    invb[l, r] = inverse
                    gb[l, r] = gain
                    new_g.append(gain)
                    new_e.append(1.0 + gain * e[r])
                e, g = tuple(new_e), tuple(new_g)
                for n in range(8):
                    field[l, n] = y[n]
            return e, g, y

        return lax.fori_loop(0, CHUNK // 5, body, carry)

    one = jnp.ones((8, 128), F32)
    carry = ((one, one), (zero, zero), (zero,) * 8)
    for part in (2, 1, 0):
        carry = eliminate_up(part, carry)
    for v in range(4):
        for r in range(2):
            surf[v * 2 + r] = xin[0, v, pl.ds(r, 8, stride=2), :] * w[r]

    def substitute(phase, part, carry, upward):
        gain, inverse = (ga, inva) if upward else (gb, invb)

        def body(i, z):
            for step in range(5):
                n = i * 5 + step
                l = part * CHUNK + (CHUNK - 1 - n if upward else n)
                z = tuple(
                    field[l, n] * inverse[l, n % 2] + gain[l, n % 2] * z[n] for n in range(8)
                )
                for n in range(8):
                    field[l, n] = z[n]
                up, down = row_pack([[z[2 * v], z[2 * v + 1]] for v in range(4)])
                up_send[phase, l] = up
                down_send[phase, l] = down
            return z

        return lax.fori_loop(0, CHUNK // 5, body, carry)

    def pack_columns(phase, part):
        def body(i, acc):
            acc = list(acc)
            for step in range(UK):
                j = i * UK + step
                l = part * CHUNK + j
                here = quad == j
                for n in range(8):
                    acc[n] = jnp.where(here, lrl(field[l, n], 4 * j + 2), acc[n])
                ends = jnp.where(even, up_send[phase, l], down_send[phase, l])
                acc[8] = jnp.where(here, lrl(ends, 4 * j + 2), acc[8])
            return tuple(acc)

        acc = lax.fori_loop(0, CHUNK // UK, body, (zero,) * 9)
        for n in range(8):
            col_send[phase, part, n] = acc[n]
        corner_send[phase, part] = acc[8]

    def message(phase, part, way):
        span = pl.ds(part * CHUNK, CHUNK)
        index = WAYS.index(way)
        if way == UP:
            src, dst = up_send.at[phase, span], up_recv.at[phase, span]
        elif way == DOWN:
            src, dst = down_send.at[phase, span], down_recv.at[phase, span]
        elif way in (RIGHT, LEFT):
            src, dst = col_send.at[phase, part], col_recv.at[index - 2, phase, part]
        else:
            src, dst = corner_send.at[phase, part], corner_recv.at[index - 4, phase, part]
        return pltpu.make_async_remote_copy(
            src_ref=src, dst_ref=dst,
            send_sem=send_sem.at[phase, part, index], recv_sem=recv_sem.at[phase, part, index],
            device_id=(ty + way[0], tx + way[1]), device_id_type=MESH,
        )

    def wet_message(way):
        index = WAYS.index(way)
        if way in (UP, DOWN):
            src, dst = wrow_send.at[index], wrow_recv.at[index]
        elif way in (RIGHT, LEFT):
            src, dst = wcol_send, wcol_recv.at[index - 2]
        else:
            src, dst = wcorner_send, wcorner_recv.at[index - 4]
        return pltpu.make_async_remote_copy(
            src_ref=src, dst_ref=dst, send_sem=wsend_sem.at[index], recv_sem=wrecv_sem.at[index],
            device_id=(ty + way[0], tx + way[1]), device_id_type=MESH,
        )

    def ctrl_message(way):
        index = WAYS.index(way)
        return pltpu.make_async_remote_copy(
            src_ref=ctrl_send.at[index], dst_ref=ctrl_recv.at[index],
            send_sem=csend_sem.at[index], recv_sem=crecv_sem.at[index],
            device_id=(ty + way[0], tx + way[1]), device_id_type=MESH,
        )

    def start(make, ways):
        for way in ways:
            @pl.when(inside(way))
            def _(way=way):
                make(way).start()

    def receive(make, ways):
        for way in ways:
            @pl.when(inside(back(way)))
            def _(way=way):
                make(way).wait_recv()

    def sent(make, ways):
        for way in ways:
            @pl.when(inside(way))
            def _(way=way):
                make(way).wait_send()

    def solve_and_send(phase, upward, ready):
        z = (zero,) * 8
        for part in ((2, 1, 0) if upward else (0, 1, 2)):
            z = substitute(phase, part, z, upward)
            if ready is not None:
                ready()
                ready = None
            start(lambda way: message(phase, part, way), WAYS[:2])
            pack_columns(phase, part)
            start(lambda way: message(phase, part, way), WAYS[2:])

    def enter():
        pl.semaphore_wait(barrier, count)
        start(wet_message, WAYS)

    solve_and_send(0, False, enter)

    kin[LEVELS] = jnp.zeros((16, 128), F32)

    def factor_body(i, e):
        for step in range(5):
            l = i * 5 + step
            new_e = []
            for r in range(2):
                k = kin[l + 1, pl.ds(r, 8, stride=2), :]
                inverse = 1.0 / (e[r] + k)
                gain = k * inverse
                inva[l, r] = inverse
                ga[l, r] = gain
                new_e.append(1.0 + gain * e[r])
            e = tuple(new_e)
        return e

    lax.fori_loop(
        0, LEVELS // 5, factor_body, tuple(1.0 + kin[0, pl.ds(r, 8, stride=2), :] for r in range(2))
    )

    for copy in small[1:]:
        copy.wait()

    shift = cols_n.bit_length() - 1
    own_row = (owner[...] >> shift) - ty
    own_col = (owner[...] & (cols_n - 1)) - tx
    cell = ((own_row + 1) * 3 + own_col + 1) * SLOTS + slot[...]
    numbers = lax.broadcasted_iota(jnp.int32, (9 * SLOTS, 128), 0)
    for row in range(16):
        hit = numbers == cell[row:row + 1, :]
        onehot[:, row * 128:(row + 1) * 128] = jnp.where(hit, 1.0, 0.0).astype(jnp.bfloat16)

    def coef_body(j, acc):
        here = quad == j
        return tuple(
            jnp.where(here, coef[v, part * CHUNK + j], acc[part * 4 + v])
            for part in range(CHUNKS) for v in range(4)
        )

    acc = lax.fori_loop(0, CHUNK, coef_body, (zero,) * (4 * CHUNKS))
    for part in range(CHUNKS):
        for v in range(4):
            c_col[part, v] = acc[part * 4 + v]

    mid = (pos == 1) | (pos == 2)
    rim_lanes = (lane < 2) | (lane >= 126)

    def neighbour_sums():
        def body(i, _):
            for step in range(UF):
                l = i * UF + step
                for v in range(4):
                    z = [field[l, 2 * v + r] for r in range(2)]
                    above, below = row_around(z[0], z[1], 0.0)
                    for r in range(2):
                        west, east = col_around(z[r], 0.0)
                        bulk[l, 2 * v + r] = (above[r] + below[r]) + (west + east)
                        if v == 2:
                            buoy[l, r] = east - west
                        if v == 3:
                            buoy[l, r] = buoy[l, r] + (below[r] - above[r])
            return 0

        lax.fori_loop(0, LEVELS // UF, body, 0)

    def inner_stencil(final):
        def body(i, _):
            for step in range(US):
                l = i * US + step
                z = [[field[l, 2 * v + r] for r in range(2)] for v in range(4)]
                for v in range(4):
                    d = [w_own[r] * bulk[l, 2 * v + r] - n_own[r] * z[v][r] for r in range(2)]
                    above, below = row_around(d[0], d[1], 0.0)
                    for r in range(2):
                        west, east = col_around(d[r], 0.0)
                        second = ((above[r] + below[r]) + (west + east)) - n_own[r] * d[r]
                        if final:
                            second = second * w_own[r]
                        value = z[v][r] - coef[v, l] * second
                        if v == 0:
                            value = value - (0.25 * THERMAL) * buoy[l, r]
                        elif v == 1:
                            value = value + (0.25 * HALINE) * buoy[l, r]
                        elif v == 2:
                            value = value - CORIOLIS * z[3][r]
                        else:
                            value = value + CORIOLIS * z[2][r]
                        bulk[l, 2 * v + r] = value
            return 0

        lax.fori_loop(0, LEVELS // US, body, 0)

    def outer_stencil(phase, part, carry, final):
        receive(lambda way: message(phase, part, way), WAYS)
        corner = corner_of(*[corner_recv[n, phase, part] for n in range(4)])
        kpack[...] = swap(corner)
        u = [
            [
                jnp.where(
                    pos < 2, col_recv[0, phase, part, 2 * v + r], col_recv[1, phase, part, 2 * v + r]
                )
                for r in range(2)
            ]
            for v in range(4)
        ]
        turned = [[swap(u[v][r]) for r in range(2)] for v in range(4)]
        for v in range(4):
            edge = srl(corner, 7 - 2 * v)
            total = packed_sum(u[v], [col_send[phase, part, 2 * v + r] for r in range(2)], edge)
            added = [jnp.where(mid, wcol_send[r] * turned[v][r], 0.0) for r in range(2)]
            above, below = row_around(added[0], added[1], 0.0)
            for r in range(2):
                outside = swap(w_col[r] * total[r] - n_col[r] * u[v][r])
                second = jnp.where(
                    mid,
                    above[r] + below[r] - n_rim[r] * added[r] + outside,
                    jnp.where(pos == 0, lrl(added[r], -1), lrl(added[r], 1)),
                )
                change = -c_col[part, v] * (wcol_send[r] * second)
                if v < 2:
                    slope = jnp.where(
                        pos == 1, turned[2][r], jnp.where(pos == 2, -turned[2][r], 0.0)
                    )
                    change = change + (-0.25 * THERMAL if v == 0 else 0.25 * HALINE) * slope
                rim[2 * v + r] = change

        def body(i, carry):
            for step in range(UC):
                m = i * UC + step
                j = CHUNK - 1 - m if final else m
                l = part * CHUNK + j
                turn = 126 - 4 * j
                line, beyond = halo_rows(
                    up_recv[phase, l], down_recv[phase, l], up_send[phase, l], down_send[phase, l]
                )
                beside = col_around(line, lrl(kpack[...], turn))
                outside = w_halo[...] * (beyond + beside[0] + beside[1]) - n_halo[...] * line
                added = w_line[...] * line
                beside = col_around(added, 0.0)
                nearest = outside + beside[0] + beside[1] - n_line[...] * added
                gains = jnp.where(
                    pair < 2,
                    jnp.where(pair == 0, coef[0, l], coef[1, l]),
                    jnp.where(pair == 2, coef[2, l], coef[3, l]),
                )
                slope = jnp.where(even, line, -line)
                slope = jnp.where(
                    pair == 0,
                    (-0.25 * THERMAL) * srl(slope, 2),
                    jnp.where(pair == 1, (0.25 * HALINE) * srl(slope, 4), 0.0),
                )
                nearest = slope - gains * (w_line[...] * nearest)
                further = -gains * (w_next[...] * added)
                new = []
                for v in range(4):
                    near = srl(nearest, 7 - 2 * v)
                    far = srl(further, 7 - 2 * v)
                    parts = (
                        jnp.where(top, near, jnp.where(bottom, far, 0.0)),
                        jnp.where(top, far, jnp.where(bottom, near, 0.0)),
                    )
                    for r in range(2):
                        n = 2 * v + r
                        new.append(
                            bulk[l, n] + parts[r] + jnp.where(rim_lanes, lrl(rim[n], turn), 0.0)
                        )
                if final:
                    for n in range(8):
                        outs[l, n // 2, pl.ds(n % 2, 8, stride=2), :] = new[n]
                else:
                    gain, y = carry
                    masked = [new[n] * w_own[n % 2] for n in range(8)]
                    y = tuple(masked[n] + gain[n % 2] * y[n] for n in range(8))
                    for n in range(8):
                        field[l, n] = y[n]
                    if part == 0 and step == 0:
                        @pl.when(i == 0)
                        def _():
                            for n in range(8):
                                surf[n] = surf[n] + masked[n]
                    carry = ((ga[l, 0], ga[l, 1]), y)
            return carry

        return lax.fori_loop(0, CHUNK // UC, body, carry)

    neighbour_sums()

    receive(wet_message, WAYS)
    wk = corner_of(wcorner_recv[0], wcorner_recv[1], wcorner_recv[2], wcorner_recv[3])
    wu2 = [jnp.where(pos < 2, wcol_recv[0, r], wcol_recv[1, r]) for r in range(2)]
    counts = packed_sum(wu2, [wcol_send[r] for r in range(2)], srl(wk, 7))
    for r in range(2):
        w_col[r] = wu2[r]
        n_col[r] = counts[r]
    line, beyond = halo_rows(wrow_recv[0], wrow_recv[1], wrow_send[0], wrow_send[1])
    beside = col_around(line, lrl(swap(wk), 126))
    w_halo[...] = line
    n_halo[...] = beyond + beside[0] + beside[1]
    above, below = row_around(w[0], w[1], srl(line, 7))
    for r in range(2):
        beside = col_around(w[r], lrl(swap(wu2[r]), 126))
        n_own[r] = above[r] + below[r] + beside[0] + beside[1]
    counts = [n_own[r] for r in range(2)]
    for r in range(2):
        n_rim[r] = tile4(counts[r])
    n_up, n_down = row_pack([counts] * 4)
    w_line[...] = jnp.where(even, srl(wd, -1), srl(wu, 1))
    n_line[...] = jnp.where(even, srl(n_down, -1), srl(n_up, 1))
    w_next[...] = jnp.where(even, wd, wu)

    inner_stencil(False)
    carry = ((zero, zero), (zero,) * 8)
    for part in range(CHUNKS):
        carry = outer_stencil(0, part, carry, False)

    solve_and_send(1, True, None)

    for v in range(4):
        for r in range(2):
            surf_rows[v, pl.ds(r, 8, stride=2), :] = surf[v * 2 + r]
    values = jnp.concatenate(
        [jnp.concatenate([surf_rows[:, row, :] for row in range(16)], axis=1)] * 2, axis=0
    )
    high = values.astype(jnp.bfloat16).astype(F32)
    rest = values - high
    middle = rest.astype(jnp.bfloat16).astype(F32)
    low = rest - middle
    pieces = jnp.concatenate([high, middle, low, low], axis=0).astype(jnp.bfloat16)
    sums = lax.dot_general(
        pieces, onehot[...], (((1,), (1,)), ((), ())), preferred_element_type=F32
    )
    sums = (sums[0:8] + sums[8:16] + sums[16:24]) * FLUX_SCALE
    near = sums[:, 0:128]
    for index, way in enumerate(WAYS):
        q = (way[0] + 1) * 3 + way[1] + 1
        if q < 8:
            ctrl_send[index] = lrl(near, -SLOTS * q)
        else:
            ctrl_send[index] = zero
            ctrl_send[index, :, 0:SLOTS] = sums[:, 128:128 + SLOTS]
    start(ctrl_message, WAYS)

    neighbour_sums()
    inner_stencil(True)

    for part in (2, 1, 0):
        outer_stencil(1, part, 0, True)

    receive(ctrl_message, WAYS)
    total = lrl(near, -SLOTS * 4)
    for index in range(8):
        total = total + ctrl_recv[index]
    sens[...] = total[0:4, 0:SLOTS]

    sent(wet_message, WAYS)
    sent(ctrl_message, WAYS)
    for phase in range(2):
        for part in range(CHUNKS):
            sent(lambda way: message(phase, part, way), WAYS)


def build(rows_n, cols_n):
    hbm = pl.BlockSpec(memory_space=pltpu.HBM)
    vmem = pl.BlockSpec(memory_space=pltpu.VMEM)
    tile = (8, 128)
    scratch = [
        pltpu.VMEM((LEVELS, 4, 16, 128), F32),
        pltpu.VMEM((LEVELS + 1, 16, 128), F32),
        pltpu.SMEM((4, LEVELS), F32),
        pltpu.VMEM((16, 128), jnp.int32),
        pltpu.VMEM((16, 128), jnp.int32),
        pltpu.VMEM((16, 128), jnp.int32),
        pltpu.VMEM((LEVELS, 8) + tile, F32),
        pltpu.VMEM((LEVELS, 8) + tile, F32),
        pltpu.VMEM((LEVELS, 2) + tile, F32),
        pltpu.VMEM((LEVELS, 2) + tile, F32),
        pltpu.VMEM((LEVELS, 2) + tile, F32),
        pltpu.VMEM((LEVELS, 2) + tile, F32),
        pltpu.VMEM((LEVELS, 2) + tile, F32),
        pltpu.VMEM((16, 128), F32),
        pltpu.VMEM((2,) + tile, F32),
        pltpu.VMEM((2,) + tile, F32),
        pltpu.VMEM(tile, F32),
        pltpu.VMEM(tile, F32),
        pltpu.VMEM((2,) + tile, F32),
        pltpu.VMEM((2,) + tile, F32),
        pltpu.VMEM((2,) + tile, F32),
        pltpu.VMEM(tile, F32),
        pltpu.VMEM(tile, F32),
        pltpu.VMEM(tile, F32),
        pltpu.VMEM((CHUNKS, 4) + tile, F32),
        pltpu.VMEM((2, LEVELS) + tile, F32),
        pltpu.VMEM((2, LEVELS) + tile, F32),
        pltpu.VMEM((2, CHUNKS, 8) + tile, F32),
        pltpu.VMEM((2, CHUNKS) + tile, F32),
        pltpu.VMEM((2, LEVELS) + tile, F32),
        pltpu.VMEM((2, LEVELS) + tile, F32),
        pltpu.VMEM((2, 2, CHUNKS, 8) + tile, F32),
        pltpu.VMEM((4, 2, CHUNKS) + tile, F32),
        pltpu.VMEM((2,) + tile, F32),
        pltpu.VMEM((2,) + tile, F32),
        pltpu.VMEM(tile, F32),
        pltpu.VMEM((2,) + tile, F32),
        pltpu.VMEM((2, 2) + tile, F32),
        pltpu.VMEM((4,) + tile, F32),
        pltpu.VMEM((8,) + tile, F32),
        pltpu.VMEM(tile, F32),
        pltpu.VMEM((8,) + tile, F32),
        pltpu.VMEM((4, 16, 128), F32),
        pltpu.VMEM((9 * SLOTS, 16 * 128), jnp.bfloat16),
        pltpu.VMEM((8,) + tile, F32),
        pltpu.VMEM((8,) + tile, F32),
        pltpu.SemaphoreType.DMA((2, CHUNKS)),
        pltpu.SemaphoreType.DMA((4,)),
        pltpu.SemaphoreType.DMA((2, CHUNKS, 8)),
        pltpu.SemaphoreType.DMA((2, CHUNKS, 8)),
        pltpu.SemaphoreType.DMA((8,)),
        pltpu.SemaphoreType.DMA((8,)),
        pltpu.SemaphoreType.DMA((8,)),
        pltpu.SemaphoreType.DMA((8,)),
    ]

    def body(*refs):
        kernel(rows_n, cols_n, *refs)

    return pl.pallas_call(
        body,
        out_shape=(pltpu.VMEM((LEVELS, 4, 16, 128), F32), pltpu.VMEM((4, SLOTS), F32)),
        in_specs=[hbm] * 6,
        out_specs=(vmem, vmem),
        scratch_shapes=scratch,
        compiler_params=pltpu.CompilerParams(
            collective_id=0, has_side_effects=True, vmem_limit_bytes=48 << 20
        ),
    )


def write_out(cotangent, sens):
    def body(x, y, x_out, y_out, sem):
        copies = [
            pltpu.make_async_copy(x, x_out, sem.at[0]),
            pltpu.make_async_copy(y, y_out, sem.at[1]),
        ]
        for copy in copies:
            copy.start()
        for copy in copies:
            copy.wait()

    place = pl.BlockSpec(memory_space=pl.ANY)
    hbm = pl.BlockSpec(memory_space=pltpu.HBM)
    return pl.pallas_call(
        body,
        out_shape=(
            jax.ShapeDtypeStruct(cotangent.shape, F32), jax.ShapeDtypeStruct(sens.shape, F32),
        ),
        in_specs=[place, place],
        out_specs=(hbm, hbm),
        scratch_shapes=[pltpu.SemaphoreType.DMA((2,))],
    )(*[pltpu.with_memory_space_constraint(a, pltpu.VMEM) for a in (cotangent, sens)])


def solution(mesh):
    def per_device(cotangent, mixing, coef, *masks):
        call = build(mesh.shape["ty"], mesh.shape["tx"])
        args = (cotangent, mixing, coef.T, *masks)
        return write_out(*call(*[pltpu.with_memory_space_constraint(a, pltpu.HBM) for a in args]))

    return jax.shard_map(
        per_device,
        mesh=mesh,
        in_specs=(
            P(None, None, "ty", "tx"),
            P(None, "ty", "tx"),
            P(),
            P("ty", "tx"),
            P("ty", "tx"),
            P("ty", "tx"),
        ),
        out_specs=(P(None, None, "ty", "tx"), P(None, ("ty", "tx"))),
        check_vma=False,
    )
```

```python
import jax
import jax.numpy as jnp
from jax import lax
from jax.experimental import pallas as pl
from jax.experimental.pallas import tpu as pltpu
from jax.sharding import PartitionSpec as P

LEVELS = 90
CHUNKS = 3
CHUNK = LEVELS // CHUNKS
SLOTS = 16
UF, US, UC, UK = 15, 15, 30, 30
MIXED = 2
OUT_PARTS = 6
THERMAL = 0.6
HALINE = 0.8
CORIOLIS = 0.3
FLUX_SCALE = 0.0625
MESH = pl.DeviceIdType.MESH
UP, DOWN, RIGHT, LEFT = (-1, 0), (1, 0), (0, 1), (0, -1)
DOWN_RIGHT, DOWN_LEFT, UP_RIGHT, UP_LEFT = (1, 1), (1, -1), (-1, 1), (-1, -1)
WAYS = (UP, DOWN, RIGHT, LEFT, DOWN_RIGHT, DOWN_LEFT, UP_RIGHT, UP_LEFT)
F32 = jnp.float32


def srl(x, shift):
    return pltpu.roll(x, shift % 8, 0)


def lrl(x, shift):
    return pltpu.roll(x, shift % 128 if isinstance(shift, int) else shift, 1)


def kernel(
    rows_n, cols_n,
    x_hbm, k_hbm, coef_hbm, wet_hbm, owner_hbm, slot_hbm,
    outs, sens,
    xin, kin, coef, wet_in, owner, slot, field, bulk, gb, invb, ga, inva, buoy, wetn, w_own, n_own,
    w_halo, n_halo, w_col, n_col, n_rim, w_line, n_line, w_next, c_col,
    up_send, down_send, col_send, corner_send, up_recv, down_recv, col_recv, corner_recv,
    wrow_send, wcol_send, wcorner_send, wrow_recv, wcol_recv, wcorner_recv,
    rim, kpack, beside_mix, surf, surf_rows, onehot, ctrl_send, ctrl_recv,
    in_sem, small_sem, send_sem, recv_sem, wsend_sem, wrecv_sem, csend_sem, crecv_sem,
):
    ty = lax.axis_index("ty")
    tx = lax.axis_index("tx")
    sub = lax.broadcasted_iota(jnp.int32, (8, 128), 0)
    lane = lax.broadcasted_iota(jnp.int32, (8, 128), 1)
    even = (sub & 1) == 0
    pair = sub >> 1
    pos = lane & 3
    quad = lane >> 2
    top, bottom = sub == 0, sub == 7
    first, last = lane == 0, lane == 127
    zero = jnp.zeros((8, 128), F32)

    def inside(way):
        row, col = ty + way[0], tx + way[1]
        return (row >= 0) & (row < rows_n) & (col >= 0) & (col < cols_n)

    def back(way):
        return (-way[0], -way[1])

    barrier = pltpu.get_barrier_semaphore()
    count = 0
    for way in WAYS:
        @pl.when(inside(way))
        def _(way=way):
            pl.semaphore_signal(
                barrier, inc=1, device_id=(ty + way[0], tx + way[1]), device_id_type=MESH
            )
        count = count + inside(way).astype(jnp.int32)

    def load(part):
        span = pl.ds(part * CHUNK, CHUNK)
        return (
            pltpu.make_async_copy(k_hbm.at[span], kin.at[span], in_sem.at[0, part]),
            pltpu.make_async_copy(x_hbm.at[span], xin.at[span], in_sem.at[1, part]),
        )

    small = [
        pltpu.make_async_copy(src, dst, small_sem.at[n])
        for n, (src, dst) in enumerate(
            ((wet_hbm, wet_in), (coef_hbm, coef), (owner_hbm, owner), (slot_hbm, slot))
        )
    ]
    small[0].start()
    for part in (2, 1, 0):
        for copy in load(part):
            copy.start()
    for copy in small[1:]:
        copy.start()

    for index, way in enumerate(WAYS):
        @pl.when(jnp.logical_not(inside(back(way))))
        def _(index=index, way=way):
            if way in (UP, DOWN):
                target = up_recv if way == UP else down_recv
                def clear(i, _):
                    for phase in range(2):
                        target[phase, i] = zero
                    return 0
                lax.fori_loop(0, LEVELS, clear, 0)
                wrow_recv[index] = zero
            elif way in (RIGHT, LEFT):
                def clear(i, _):
                    for phase in range(2):
                        for c in range(CHUNKS):
                            col_recv[index - 2, phase, c, i] = zero
                    return 0
                lax.fori_loop(0, 8, clear, 0)
                for r in range(2):
                    wcol_recv[index - 2, r] = zero
            else:
                for phase in range(2):
                    for c in range(CHUNKS):
                        corner_recv[index - 4, phase, c] = zero
                wcorner_recv[index - 4] = zero
            ctrl_recv[index] = zero

    def row_pack(x):
        q = []
        for r in range(2):
            acc = srl(x[0][r], 1)
            for v in range(1, 4):
                acc = jnp.where(pair == v, srl(x[v][r], 2 * v + 1), acc)
            q.append(acc)
        return jnp.where(even, srl(q[0], -1), q[1]), jnp.where(even, q[0], srl(q[1], 1))

    def row_around(x0, x1, edge):
        return (
            (jnp.where(top, edge, srl(x1, 1)), x0),
            (x1, jnp.where(bottom, edge, srl(x0, -1))),
        )

    def col_around(x, edge):
        return jnp.where(first, edge, lrl(x, 1)), jnp.where(last, edge, lrl(x, -1))

    def swap(x):
        return jnp.where(pos == 1, lrl(x, -1), lrl(x, 1))

    def corner_of(ul, ur, dl, dr):
        return jnp.where(even, jnp.where(pos < 2, dl, dr), jnp.where(pos < 2, ul, ur))

    def packed_sum(u, own, edge):
        above, below = row_around(u[0], u[1], edge)
        result = []
        for r in range(2):
            e = jnp.where(pos < 2, u[r], own[r])
            f = jnp.where(pos < 2, own[r], u[r])
            beside = jnp.where(pos < 2, lrl(e, 1) + lrl(e, -1), lrl(f, 1) + lrl(f, -1))
            result.append(beside + above[r] + below[r])
        return result

    def halo_rows(up_r, down_r, up_s, down_s):
        line = jnp.where(even, up_r, down_r)
        beyond = jnp.where(even, srl(up_r + down_s, -1), srl(down_r + up_s, 1))
        return line, beyond

    small[0].wait()
    wetn[...] = wet_in[...].astype(F32)
    w = [wetn[pl.ds(r, 8, stride=2), :] for r in range(2)]
    for r in range(2):
        w_own[r] = w[r]

    def tile4(x):
        x = jnp.where(lane < 4, lrl(x, 2), 0.0)
        for step in (4, 8, 16, 32, 64):
            x = x + lrl(x, step)
        return x

    wu, wd = row_pack([w] * 4)
    wrow_send[0] = wu
    wrow_send[1] = wd
    for r in range(2):
        wcol_send[r] = tile4(w[r])
    wcorner_send[...] = tile4(jnp.where(even, wu, wd))

    def eliminate_up(part, carry):
        for copy in load(part):
            copy.wait()

        def body(i, carry):
            e, g, y = carry
            above, below = list(e), [one, one]
            for step in range(5):
                l = part * CHUNK + CHUNK - 1 - (i * 5 + step)
                masked = [
                    [xin[l, v, pl.ds(r, 8, stride=2), :] * w[r] for r in range(2)] for v in range(4)
                ]
                y = tuple(
                    masked[v][r] + g[r] * y[v * 2 + r] for v in range(4) for r in range(2)
                )
                new_g, scale = [], []
                for r in range(2):
                    k = kin[l, pl.ds(r, 8, stride=2), :]
                    coupled = k * below[r]
                    grown = above[r] + coupled
                    scale.append(1.0 / grown)
                    gain = coupled * scale[r]
                    invb[l, r] = below[r] * scale[r]
                    gb[l, r] = gain
                    new_g.append(gain)
                    above[r] = grown + k * above[r]
                    below[r] = grown
                g = tuple(new_g)
                for n in range(8):
                    field[l, n] = y[n]
            return tuple(above[r] * scale[r] for r in range(2)), g, y

        return lax.fori_loop(0, CHUNK // 5, body, carry)

    one = jnp.ones((8, 128), F32)
    carry = ((one, one), (zero, zero), (zero,) * 8)
    for part in (2, 1, 0):
        carry = eliminate_up(part, carry)
    for v in range(4):
        for r in range(2):
            surf[v * 2 + r] = xin[0, v, pl.ds(r, 8, stride=2), :] * w[r]

    def substitute(phase, part, carry, upward):
        gain, inverse = (ga, inva) if upward else (gb, invb)

        def body(i, z):
            for step in range(5):
                n = i * 5 + step
                l = part * CHUNK + (CHUNK - 1 - n if upward else n)
                z = tuple(
                    field[l, n] * inverse[l, n % 2] + gain[l, n % 2] * z[n] for n in range(8)
                )
                for n in range(8):
                    field[l, n] = z[n]
                up, down = row_pack([[z[2 * v], z[2 * v + 1]] for v in range(4)])
                up_send[phase, l] = up
                down_send[phase, l] = down
            return z

        return lax.fori_loop(0, CHUNK // 5, body, carry)

    def pack_columns(phase, part):
        def body(i, acc):
            acc = list(acc)
            for step in range(UK):
                j = i * UK + step
                l = part * CHUNK + j
                here = quad == j
                for n in range(8):
                    acc[n] = jnp.where(here, lrl(field[l, n], 4 * j + 2), acc[n])
                ends = jnp.where(even, up_send[phase, l], down_send[phase, l])
                acc[8] = jnp.where(here, lrl(ends, 4 * j + 2), acc[8])
            return tuple(acc)

        acc = lax.fori_loop(0, CHUNK // UK, body, (zero,) * 9)
        for n in range(8):
            col_send[phase, part, n] = acc[n]
        corner_send[phase, part] = acc[8]

    def message(phase, part, way):
        span = pl.ds(part * CHUNK, CHUNK)
        index = WAYS.index(way)
        if way == UP:
            src, dst = up_send.at[phase, span], up_recv.at[phase, span]
        elif way == DOWN:
            src, dst = down_send.at[phase, span], down_recv.at[phase, span]
        elif way in (RIGHT, LEFT):
            src, dst = col_send.at[phase, part], col_recv.at[index - 2, phase, part]
        else:
            src, dst = corner_send.at[phase, part], corner_recv.at[index - 4, phase, part]
        return pltpu.make_async_remote_copy(
            src_ref=src, dst_ref=dst,
            send_sem=send_sem.at[phase, part, index], recv_sem=recv_sem.at[phase, part, index],
            device_id=(ty + way[0], tx + way[1]), device_id_type=MESH,
        )

    def wet_message(way):
        index = WAYS.index(way)
        if way in (UP, DOWN):
            src, dst = wrow_send.at[index], wrow_recv.at[index]
        elif way in (RIGHT, LEFT):
            src, dst = wcol_send, wcol_recv.at[index - 2]
        else:
            src, dst = wcorner_send, wcorner_recv.at[index - 4]
        return pltpu.make_async_remote_copy(
            src_ref=src, dst_ref=dst, send_sem=wsend_sem.at[index], recv_sem=wrecv_sem.at[index],
            device_id=(ty + way[0], tx + way[1]), device_id_type=MESH,
        )

    def ctrl_message(way):
        index = WAYS.index(way)
        return pltpu.make_async_remote_copy(
            src_ref=ctrl_send.at[index], dst_ref=ctrl_recv.at[index],
            send_sem=csend_sem.at[index], recv_sem=crecv_sem.at[index],
            device_id=(ty + way[0], tx + way[1]), device_id_type=MESH,
        )

    def start(make, ways):
        for way in ways:
            @pl.when(inside(way))
            def _(way=way):
                make(way).start()

    def receive(make, ways):
        for way in ways:
            @pl.when(inside(back(way)))
            def _(way=way):
                make(way).wait_recv()

    def sent(make, ways):
        for way in ways:
            @pl.when(inside(way))
            def _(way=way):
                make(way).wait_send()

    def solve_and_send(phase, upward, ready):
        z = (zero,) * 8
        for part in ((2, 1, 0) if upward else (0, 1, 2)):
            z = substitute(phase, part, z, upward)
            if ready is not None:
                ready()
                ready = None
            start(lambda way: message(phase, part, way), WAYS[:2])
            pack_columns(phase, part)
            start(lambda way: message(phase, part, way), WAYS[2:])

    def enter():
        pl.semaphore_wait(barrier, count)
        start(wet_message, WAYS)

    kin[LEVELS] = jnp.zeros((16, 128), F32)

    def factor_body(i, e):
        above, below = list(e), [one, one]
        for step in range(5):
            l = i * 5 + step
            scale = []
            for r in range(2):
                k = kin[l + 1, pl.ds(r, 8, stride=2), :]
                coupled = k * below[r]
                grown = above[r] + coupled
                scale.append(1.0 / grown)
                inva[l, r] = below[r] * scale[r]
                ga[l, r] = coupled * scale[r]
                above[r] = grown + k * above[r]
                below[r] = grown
        return tuple(above[r] * scale[r] for r in range(2))

    lax.fori_loop(
        0, LEVELS // 5, factor_body, tuple(1.0 + kin[0, pl.ds(r, 8, stride=2), :] for r in range(2))
    )

    solve_and_send(0, False, enter)

    for copy in small[1:]:
        copy.wait()

    shift = cols_n.bit_length() - 1
    own_row = (owner[...] >> shift) - ty
    own_col = (owner[...] & (cols_n - 1)) - tx
    cell = ((own_row + 1) * 3 + own_col + 1) * SLOTS + slot[...]
    numbers = lax.broadcasted_iota(jnp.int32, (9 * SLOTS, 128), 0)
    for row in range(16):
        hit = numbers == cell[row:row + 1, :]
        onehot[:, row * 128:(row + 1) * 128] = jnp.where(hit, 1.0, 0.0).astype(jnp.bfloat16)

    def coef_body(j, acc):
        here = quad == j
        return tuple(
            jnp.where(here, coef[v, part * CHUNK + j], acc[part * 4 + v])
            for part in range(CHUNKS) for v in range(4)
        )

    acc = lax.fori_loop(0, CHUNK, coef_body, (zero,) * (4 * CHUNKS))
    for part in range(CHUNKS):
        for v in range(4):
            c_col[part, v] = acc[part * 4 + v]

    source = lax.broadcasted_iota(jnp.int32, (256, 128), 0) & 127
    target = lax.broadcasted_iota(jnp.int32, (256, 128), 1)
    beside_mix[...] = jnp.where(
        (source == target - 1) | (source == target + 1), 1.0, 0.0
    ).astype(jnp.bfloat16)


    mid = (pos == 1) | (pos == 2)
    rim_lanes = (lane < 2) | (lane >= 126)

    def beside_product(levels):
        x = jnp.concatenate([x for level in levels for x in level[:2 * MIXED]], axis=0)
        high = x.astype(jnp.bfloat16)
        both = jnp.concatenate([high, (x - high.astype(F32)).astype(jnp.bfloat16)], axis=1)
        y = jnp.dot(both, beside_mix[...], preferred_element_type=F32)
        return lambda step, n: y[16 * MIXED * step + 8 * n:16 * MIXED * step + 8 * n + 8]

    def neighbour_sums():
        def body(i, _):
            z = [[field[i * UF + step, n] for n in range(8)] for step in range(UF)]
            product = beside_product(z)
            for step in range(UF):
                l = i * UF + step
                for v in range(4):
                    above, below = row_around(z[step][2 * v], z[step][2 * v + 1], 0.0)
                    for r in range(2):
                        n = 2 * v + r
                        if v < MIXED:
                            beside = product(step, n)
                        else:
                            west, east = col_around(z[step][n], 0.0)
                            beside = west + east
                        bulk[l, n] = (above[r] + below[r]) + beside
                        if v == 2:
                            buoy[l, r] = east - west
                        if v == 3:
                            buoy[l, r] = buoy[l, r] + (below[r] - above[r])
            return 0

        lax.fori_loop(0, LEVELS // UF, body, 0)

    def inner_stencil(final):
        def body(i, _):
            d = [
                [
                    w_own[n % 2] * bulk[i * US + step, n] - n_own[n % 2] * field[i * US + step, n]
                    for n in range(8)
                ]
                for step in range(US)
            ]
            product = beside_product(d)
            for step in range(US):
                l = i * US + step
                z = [[field[l, 2 * v + r] for r in range(2)] for v in range(4)]
                for v in range(4):
                    above, below = row_around(d[step][2 * v], d[step][2 * v + 1], 0.0)
                    for r in range(2):
                        n = 2 * v + r
                        if v < MIXED:
                            beside = product(step, n)
                        else:
                            west, east = col_around(d[step][n], 0.0)
                            beside = west + east
                        second = ((above[r] + below[r]) + beside) - n_own[r] * d[step][n]
                        if final:
                            second = second * w_own[r]
                        value = z[v][r] - coef[v, l] * second
                        if v == 0:
                            value = value - (0.25 * THERMAL) * buoy[l, r]
                        elif v == 1:
                            value = value + (0.25 * HALINE) * buoy[l, r]
                        elif v == 2:
                            value = value - CORIOLIS * z[3][r]
                        else:
                            value = value + CORIOLIS * z[2][r]
                        bulk[l, n] = value
            return 0

        lax.fori_loop(0, LEVELS // US, body, 0)

    def outer_stencil(phase, part, carry, final):
        receive(lambda way: message(phase, part, way), WAYS)
        corner = corner_of(*[corner_recv[n, phase, part] for n in range(4)])
        kpack[...] = swap(corner)
        u = [
            [
                jnp.where(
                    pos < 2, col_recv[0, phase, part, 2 * v + r], col_recv[1, phase, part, 2 * v + r]
                )
                for r in range(2)
            ]
            for v in range(4)
        ]
        turned = [[swap(u[v][r]) for r in range(2)] for v in range(4)]
        for v in range(4):
            edge = srl(corner, 7 - 2 * v)
            total = packed_sum(u[v], [col_send[phase, part, 2 * v + r] for r in range(2)], edge)
            added = [jnp.where(mid, wcol_send[r] * turned[v][r], 0.0) for r in range(2)]
            above, below = row_around(added[0], added[1], 0.0)
            for r in range(2):
                outside = swap(w_col[r] * total[r] - n_col[r] * u[v][r])
                second = jnp.where(
                    mid,
                    above[r] + below[r] - n_rim[r] * added[r] + outside,
                    jnp.where(pos == 0, lrl(added[r], -1), lrl(added[r], 1)),
                )
                change = -c_col[part, v] * (wcol_send[r] * second)
                if v < 2:
                    slope = jnp.where(
                        pos == 1, turned[2][r], jnp.where(pos == 2, -turned[2][r], 0.0)
                    )
                    change = change + (-0.25 * THERMAL if v == 0 else 0.25 * HALINE) * slope
                rim[2 * v + r] = change

        def body(i, carry):
            for step in range(UC):
                m = i * UC + step
                j = CHUNK - 1 - m if final else m
                l = part * CHUNK + j
                turn = 126 - 4 * j
                line, beyond = halo_rows(
                    up_recv[phase, l], down_recv[phase, l], up_send[phase, l], down_send[phase, l]
                )
                beside = col_around(line, lrl(kpack[...], turn))
                outside = w_halo[...] * (beyond + beside[0] + beside[1]) - n_halo[...] * line
                added = w_line[...] * line
                beside = col_around(added, 0.0)
                nearest = outside + beside[0] + beside[1] - n_line[...] * added
                gains = jnp.where(
                    pair < 2,
                    jnp.where(pair == 0, coef[0, l], coef[1, l]),
                    jnp.where(pair == 2, coef[2, l], coef[3, l]),
                )
                slope = jnp.where(even, line, -line)
                slope = jnp.where(
                    pair == 0,
                    (-0.25 * THERMAL) * srl(slope, 2),
                    jnp.where(pair == 1, (0.25 * HALINE) * srl(slope, 4), 0.0),
                )
                nearest = slope - gains * (w_line[...] * nearest)
                further = -gains * (w_next[...] * added)
                new = []
                for v in range(4):
                    near = srl(nearest, 7 - 2 * v)
                    far = srl(further, 7 - 2 * v)
                    parts = (
                        jnp.where(top, near, jnp.where(bottom, far, 0.0)),
                        jnp.where(top, far, jnp.where(bottom, near, 0.0)),
                    )
                    for r in range(2):
                        n = 2 * v + r
                        new.append(
                            bulk[l, n] + parts[r] + jnp.where(rim_lanes, lrl(rim[n], turn), 0.0)
                        )
                if final:
                    for n in range(8):
                        outs[l, n // 2, pl.ds(n % 2, 8, stride=2), :] = new[n]
                else:
                    gain, y = carry
                    masked = [new[n] * w_own[n % 2] for n in range(8)]
                    y = tuple(masked[n] + gain[n % 2] * y[n] for n in range(8))
                    for n in range(8):
                        field[l, n] = y[n]
                    if part == 0 and step == 0:
                        @pl.when(i == 0)
                        def _():
                            for n in range(8):
                                surf[n] = surf[n] + masked[n]
                    carry = ((ga[l, 0], ga[l, 1]), y)
            return carry

        return lax.fori_loop(0, CHUNK // UC, body, carry)

    neighbour_sums()

    receive(wet_message, WAYS)
    wk = corner_of(wcorner_recv[0], wcorner_recv[1], wcorner_recv[2], wcorner_recv[3])
    wu2 = [jnp.where(pos < 2, wcol_recv[0, r], wcol_recv[1, r]) for r in range(2)]
    counts = packed_sum(wu2, [wcol_send[r] for r in range(2)], srl(wk, 7))
    for r in range(2):
        w_col[r] = wu2[r]
        n_col[r] = counts[r]
    line, beyond = halo_rows(wrow_recv[0], wrow_recv[1], wrow_send[0], wrow_send[1])
    beside = col_around(line, lrl(swap(wk), 126))
    w_halo[...] = line
    n_halo[...] = beyond + beside[0] + beside[1]
    above, below = row_around(w[0], w[1], srl(line, 7))
    for r in range(2):
        beside = col_around(w[r], lrl(swap(wu2[r]), 126))
        n_own[r] = above[r] + below[r] + beside[0] + beside[1]
    counts = [n_own[r] for r in range(2)]
    for r in range(2):
        n_rim[r] = tile4(counts[r])
    n_up, n_down = row_pack([counts] * 4)
    w_line[...] = jnp.where(even, srl(wd, -1), srl(wu, 1))
    n_line[...] = jnp.where(even, srl(n_down, -1), srl(n_up, 1))
    w_next[...] = jnp.where(even, wd, wu)

    inner_stencil(False)
    carry = ((zero, zero), (zero,) * 8)
    for part in range(CHUNKS):
        carry = outer_stencil(0, part, carry, False)

    solve_and_send(1, True, None)

    for v in range(4):
        for r in range(2):
            surf_rows[v, pl.ds(r, 8, stride=2), :] = surf[v * 2 + r]
    values = jnp.concatenate(
        [jnp.concatenate([surf_rows[:, row, :] for row in range(16)], axis=1)] * 2, axis=0
    )
    high = values.astype(jnp.bfloat16).astype(F32)
    rest = values - high
    middle = rest.astype(jnp.bfloat16).astype(F32)
    low = rest - middle
    pieces = jnp.concatenate([high, middle, low, low], axis=0).astype(jnp.bfloat16)
    sums = lax.dot_general(
        pieces, onehot[...], (((1,), (1,)), ((), ())), preferred_element_type=F32
    )
    sums = (sums[0:8] + sums[8:16] + sums[16:24]) * FLUX_SCALE
    near = sums[:, 0:128]
    for index, way in enumerate(WAYS):
        q = (way[0] + 1) * 3 + way[1] + 1
        if q < 8:
            ctrl_send[index] = lrl(near, -SLOTS * q)
        else:
            ctrl_send[index] = zero
            ctrl_send[index, :, 0:SLOTS] = sums[:, 128:128 + SLOTS]
    start(ctrl_message, WAYS)

    neighbour_sums()
    inner_stencil(True)

    for part in (2, 1, 0):
        outer_stencil(1, part, 0, True)

    receive(ctrl_message, WAYS)
    total = lrl(near, -SLOTS * 4)
    for index in range(8):
        total = total + ctrl_recv[index]
    sens[...] = total[0:4, 0:SLOTS]

    sent(wet_message, WAYS)
    sent(ctrl_message, WAYS)
    for phase in range(2):
        for part in range(CHUNKS):
            sent(lambda way: message(phase, part, way), WAYS)


def build(rows_n, cols_n):
    hbm = pl.BlockSpec(memory_space=pltpu.HBM)
    vmem = pl.BlockSpec(memory_space=pltpu.VMEM)
    tile = (8, 128)
    scratch = [
        pltpu.VMEM((LEVELS, 4, 16, 128), F32),
        pltpu.VMEM((LEVELS + 1, 16, 128), F32),
        pltpu.SMEM((4, LEVELS), F32),
        pltpu.VMEM((16, 128), jnp.int32),
        pltpu.VMEM((16, 128), jnp.int32),
        pltpu.VMEM((16, 128), jnp.int32),
        pltpu.VMEM((LEVELS, 8) + tile, F32),
        pltpu.VMEM((LEVELS, 8) + tile, F32),
        pltpu.VMEM((LEVELS, 2) + tile, F32),
        pltpu.VMEM((LEVELS, 2) + tile, F32),
        pltpu.VMEM((LEVELS, 2) + tile, F32),
        pltpu.VMEM((LEVELS, 2) + tile, F32),
        pltpu.VMEM((LEVELS, 2) + tile, F32),
        pltpu.VMEM((16, 128), F32),
        pltpu.VMEM((2,) + tile, F32),
        pltpu.VMEM((2,) + tile, F32),
        pltpu.VMEM(tile, F32),
        pltpu.VMEM(tile, F32),
        pltpu.VMEM((2,) + tile, F32),
        pltpu.VMEM((2,) + tile, F32),
        pltpu.VMEM((2,) + tile, F32),
        pltpu.VMEM(tile, F32),
        pltpu.VMEM(tile, F32),
        pltpu.VMEM(tile, F32),
        pltpu.VMEM((CHUNKS, 4) + tile, F32),
        pltpu.VMEM((2, LEVELS) + tile, F32),
        pltpu.VMEM((2, LEVELS) + tile, F32),
        pltpu.VMEM((2, CHUNKS, 8) + tile, F32),
        pltpu.VMEM((2, CHUNKS) + tile, F32),
        pltpu.VMEM((2, LEVELS) + tile, F32),
        pltpu.VMEM((2, LEVELS) + tile, F32),
        pltpu.VMEM((2, 2, CHUNKS, 8) + tile, F32),
        pltpu.VMEM((4, 2, CHUNKS) + tile, F32),
        pltpu.VMEM((2,) + tile, F32),
        pltpu.VMEM((2,) + tile, F32),
        pltpu.VMEM(tile, F32),
        pltpu.VMEM((2,) + tile, F32),
        pltpu.VMEM((2, 2) + tile, F32),
        pltpu.VMEM((4,) + tile, F32),
        pltpu.VMEM((8,) + tile, F32),
        pltpu.VMEM(tile, F32),
        pltpu.VMEM((256, 128), jnp.bfloat16),
        pltpu.VMEM((8,) + tile, F32),
        pltpu.VMEM((4, 16, 128), F32),
        pltpu.VMEM((9 * SLOTS, 16 * 128), jnp.bfloat16),
        pltpu.VMEM((8,) + tile, F32),
        pltpu.VMEM((8,) + tile, F32),
        pltpu.SemaphoreType.DMA((2, CHUNKS)),
        pltpu.SemaphoreType.DMA((4,)),
        pltpu.SemaphoreType.DMA((2, CHUNKS, 8)),
        pltpu.SemaphoreType.DMA((2, CHUNKS, 8)),
        pltpu.SemaphoreType.DMA((8,)),
        pltpu.SemaphoreType.DMA((8,)),
        pltpu.SemaphoreType.DMA((8,)),
        pltpu.SemaphoreType.DMA((8,)),
    ]

    def body(*refs):
        kernel(rows_n, cols_n, *refs)

    return pl.pallas_call(
        body,
        out_shape=(pltpu.VMEM((LEVELS, 4, 16, 128), F32), pltpu.VMEM((4, SLOTS), F32)),
        in_specs=[hbm] * 6,
        out_specs=(vmem, vmem),
        scratch_shapes=scratch,
        compiler_params=pltpu.CompilerParams(
            collective_id=0, has_side_effects=True, vmem_limit_bytes=48 << 20
        ),
    )


def write_out(cotangent, sens):
    def body(x, y, x_out, y_out, sem):
        span = LEVELS // OUT_PARTS
        copies = [
            pltpu.make_async_copy(
                x.at[pl.ds(n * span, span)], x_out.at[pl.ds(n * span, span)], sem.at[n]
            )
            for n in range(OUT_PARTS)
        ]
        copies.append(pltpu.make_async_copy(y, y_out, sem.at[OUT_PARTS]))
        for copy in copies:
            copy.start()
        for copy in copies:
            copy.wait()

    place = pl.BlockSpec(memory_space=pl.ANY)
    hbm = pl.BlockSpec(memory_space=pltpu.HBM)
    return pl.pallas_call(
        body,
        out_shape=(
            jax.ShapeDtypeStruct(cotangent.shape, F32), jax.ShapeDtypeStruct(sens.shape, F32),
        ),
        in_specs=[place, place],
        out_specs=(hbm, hbm),
        scratch_shapes=[pltpu.SemaphoreType.DMA((OUT_PARTS + 1,))],
    )(*[pltpu.with_memory_space_constraint(a, pltpu.VMEM) for a in (cotangent, sens)])


def solution(mesh):
    def per_device(cotangent, mixing, coef, *masks):
        call = build(mesh.shape["ty"], mesh.shape["tx"])
        args = (cotangent, mixing, coef.T, *masks)
        return write_out(*call(*[pltpu.with_memory_space_constraint(a, pltpu.HBM) for a in args]))

    return jax.shard_map(
        per_device,
        mesh=mesh,
        in_specs=(
            P(None, None, "ty", "tx"),
            P(None, "ty", "tx"),
            P(),
            P("ty", "tx"),
            P("ty", "tx"),
            P("ty", "tx"),
        ),
        out_specs=(P(None, None, "ty", "tx"), P(None, ("ty", "tx"))),
        check_vma=False,
    )
```

```python
import jax
import jax.numpy as jnp
from jax import lax
from jax.experimental import pallas as pl
from jax.experimental.pallas import tpu as pltpu
from jax.sharding import PartitionSpec as P

LEVELS = 90
CHUNKS = 3
CHUNK = LEVELS // CHUNKS
SLOTS = 16
UF, US, UC, UK = 15, 15, 30, 30
MIXED = 2
OUT_PARTS = 6
THERMAL = 0.6
HALINE = 0.8
CORIOLIS = 0.3
FLUX_SCALE = 0.0625
MESH = pl.DeviceIdType.MESH
UP, DOWN, RIGHT, LEFT = (-1, 0), (1, 0), (0, 1), (0, -1)
DOWN_RIGHT, DOWN_LEFT, UP_RIGHT, UP_LEFT = (1, 1), (1, -1), (-1, 1), (-1, -1)
WAYS = (UP, DOWN, RIGHT, LEFT, DOWN_RIGHT, DOWN_LEFT, UP_RIGHT, UP_LEFT)
F32 = jnp.float32


def srl(x, shift):
    return pltpu.roll(x, shift % 8, 0)


def lrl(x, shift):
    return pltpu.roll(x, shift % 128 if isinstance(shift, int) else shift, 1)


def kernel(
    rows_n, cols_n,
    x_hbm, k_hbm, coef_hbm, wet_hbm, owner_hbm, slot_hbm,
    outs, sens,
    xin, kin, coef, wet_in, owner, slot, field, bulk, gb, invb, ga, inva, buoy, wetn, w_own, n_own,
    w_halo, n_halo, w_col, n_col, n_rim, w_line, n_line, w_next, c_col,
    up_send, down_send, col_send, corner_send, up_recv, down_recv, col_recv, corner_recv,
    wrow_send, wcol_send, wcorner_send, wrow_recv, wcol_recv, wcorner_recv,
    rim, kpack, beside_mix, surf, surf_rows, onehot, ctrl_send, ctrl_recv,
    in_sem, small_sem, send_sem, recv_sem, wsend_sem, wrecv_sem, csend_sem, crecv_sem,
):
    ty = lax.axis_index("ty")
    tx = lax.axis_index("tx")
    sub = lax.broadcasted_iota(jnp.int32, (8, 128), 0)
    lane = lax.broadcasted_iota(jnp.int32, (8, 128), 1)
    even = (sub & 1) == 0
    pair = sub >> 1
    pos = lane & 3
    quad = lane >> 2
    top, bottom = sub == 0, sub == 7
    first, last = lane == 0, lane == 127
    zero = jnp.zeros((8, 128), F32)

    def inside(way):
        row, col = ty + way[0], tx + way[1]
        return (row >= 0) & (row < rows_n) & (col >= 0) & (col < cols_n)

    def back(way):
        return (-way[0], -way[1])

    barrier = pltpu.get_barrier_semaphore()
    count = 0
    for way in WAYS:
        @pl.when(inside(way))
        def _(way=way):
            pl.semaphore_signal(
                barrier, inc=1, device_id=(ty + way[0], tx + way[1]), device_id_type=MESH
            )
        count = count + inside(way).astype(jnp.int32)

    def load(part):
        span = pl.ds(part * CHUNK, CHUNK)
        return (
            pltpu.make_async_copy(k_hbm.at[span], kin.at[span], in_sem.at[0, part]),
            pltpu.make_async_copy(x_hbm.at[span], xin.at[span], in_sem.at[1, part]),
        )

    small = [
        pltpu.make_async_copy(src, dst, small_sem.at[n])
        for n, (src, dst) in enumerate(
            ((wet_hbm, wet_in), (coef_hbm, coef), (owner_hbm, owner), (slot_hbm, slot))
        )
    ]
    small[0].start()
    for part in (2, 1, 0):
        for copy in load(part):
            copy.start()
    for copy in small[1:]:
        copy.start()

    def row_pack(x):
        q = []
        for r in range(2):
            acc = srl(x[0][r], 1)
            for v in range(1, 4):
                acc = jnp.where(pair == v, srl(x[v][r], 2 * v + 1), acc)
            q.append(acc)
        return jnp.where(even, srl(q[0], -1), q[1]), jnp.where(even, q[0], srl(q[1], 1))

    def row_around(x0, x1, edge):
        return (
            (jnp.where(top, edge, srl(x1, 1)), x0),
            (x1, jnp.where(bottom, edge, srl(x0, -1))),
        )

    def col_around(x, edge):
        return jnp.where(first, edge, lrl(x, 1)), jnp.where(last, edge, lrl(x, -1))

    def swap(x):
        return jnp.where(pos == 1, lrl(x, -1), lrl(x, 1))

    def corner_of(ul, ur, dl, dr):
        return jnp.where(even, jnp.where(pos < 2, dl, dr), jnp.where(pos < 2, ul, ur))

    def packed_sum(u, own, edge):
        above, below = row_around(u[0], u[1], edge)
        result = []
        for r in range(2):
            e = jnp.where(pos < 2, u[r], own[r])
            f = jnp.where(pos < 2, own[r], u[r])
            beside = jnp.where(pos < 2, lrl(e, 1) + lrl(e, -1), lrl(f, 1) + lrl(f, -1))
            result.append(beside + above[r] + below[r])
        return result

    def halo_rows(up_r, down_r, up_s, down_s):
        line = jnp.where(even, up_r, down_r)
        beyond = jnp.where(even, srl(up_r + down_s, -1), srl(down_r + up_s, 1))
        return line, beyond

    small[0].wait()
    wetn[...] = wet_in[...].astype(F32)
    w = [wetn[pl.ds(r, 8, stride=2), :] for r in range(2)]
    for r in range(2):
        w_own[r] = w[r]

    spread = jnp.where(
        lax.broadcasted_iota(jnp.int32, (128, 128), 0)
        == ((126 + (lax.broadcasted_iota(jnp.int32, (128, 128), 1) & 3)) & 127),
        1.0, 0.0,
    ).astype(jnp.bfloat16)

    def tile4(x):
        return jnp.dot(x.astype(jnp.bfloat16), spread, preferred_element_type=F32)

    wu, wd = row_pack([w] * 4)
    wrow_send[0] = wu
    wrow_send[1] = wd
    for r in range(2):
        wcol_send[r] = tile4(w[r])
    wcorner_send[...] = tile4(jnp.where(even, wu, wd))

    def eliminate_up(part, carry):
        for copy in load(part):
            copy.wait()

        def body(i, carry):
            e, g, y = carry
            above, below = list(e), [one, one]
            for step in range(5):
                l = part * CHUNK + CHUNK - 1 - (i * 5 + step)
                masked = [
                    [xin[l, v, pl.ds(r, 8, stride=2), :] * w[r] for r in range(2)] for v in range(4)
                ]
                y = tuple(
                    masked[v][r] + g[r] * y[v * 2 + r] for v in range(4) for r in range(2)
                )
                new_g, scale = [], []
                for r in range(2):
                    k = kin[l, pl.ds(r, 8, stride=2), :]
                    coupled = k * below[r]
                    grown = above[r] + coupled
                    scale.append(1.0 / grown)
                    gain = coupled * scale[r]
                    invb[l, r] = below[r] * scale[r]
                    gb[l, r] = gain
                    new_g.append(gain)
                    above[r] = grown + k * above[r]
                    below[r] = grown
                g = tuple(new_g)
                for n in range(8):
                    field[l, n] = y[n]
            return tuple(above[r] * scale[r] for r in range(2)), g, y

        return lax.fori_loop(0, CHUNK // 5, body, carry)

    one = jnp.ones((8, 128), F32)
    carry = ((one, one), (zero, zero), (zero,) * 8)
    for part in (2, 1, 0):
        carry = eliminate_up(part, carry)
    for v in range(4):
        for r in range(2):
            surf[v * 2 + r] = xin[0, v, pl.ds(r, 8, stride=2), :] * w[r]

    def substitute(phase, part, carry, upward):
        gain, inverse = (ga, inva) if upward else (gb, invb)

        def body(i, z):
            for step in range(5):
                n = i * 5 + step
                l = part * CHUNK + (CHUNK - 1 - n if upward else n)
                z = tuple(
                    field[l, n] * inverse[l, n % 2] + gain[l, n % 2] * z[n] for n in range(8)
                )
                for n in range(8):
                    field[l, n] = z[n]
                up, down = row_pack([[z[2 * v], z[2 * v + 1]] for v in range(4)])
                up_send[phase, l] = up
                down_send[phase, l] = down
            return z

        return lax.fori_loop(0, CHUNK // 5, body, carry)

    def pack_columns(phase, part):
        def body(i, acc):
            acc = list(acc)
            for step in range(UK):
                j = i * UK + step
                l = part * CHUNK + j
                here = quad == j
                for n in range(8):
                    acc[n] = jnp.where(here, lrl(field[l, n], 4 * j + 2), acc[n])
                ends = jnp.where(even, up_send[phase, l], down_send[phase, l])
                acc[8] = jnp.where(here, lrl(ends, 4 * j + 2), acc[8])
            return tuple(acc)

        acc = lax.fori_loop(0, CHUNK // UK, body, (zero,) * 9)
        for n in range(8):
            col_send[phase, part, n] = acc[n]
        corner_send[phase, part] = acc[8]

    def message(phase, part, way):
        span = pl.ds(part * CHUNK, CHUNK)
        index = WAYS.index(way)
        if way == UP:
            src, dst = up_send.at[phase, span], up_recv.at[phase, span]
        elif way == DOWN:
            src, dst = down_send.at[phase, span], down_recv.at[phase, span]
        elif way in (RIGHT, LEFT):
            src, dst = col_send.at[phase, part], col_recv.at[index - 2, phase, part]
        else:
            src, dst = corner_send.at[phase, part], corner_recv.at[index - 4, phase, part]
        return pltpu.make_async_remote_copy(
            src_ref=src, dst_ref=dst,
            send_sem=send_sem.at[phase, part, index], recv_sem=recv_sem.at[phase, part, index],
            device_id=(ty + way[0], tx + way[1]), device_id_type=MESH,
        )

    def wet_message(way):
        index = WAYS.index(way)
        if way in (UP, DOWN):
            src, dst = wrow_send.at[index], wrow_recv.at[index]
        elif way in (RIGHT, LEFT):
            src, dst = wcol_send, wcol_recv.at[index - 2]
        else:
            src, dst = wcorner_send, wcorner_recv.at[index - 4]
        return pltpu.make_async_remote_copy(
            src_ref=src, dst_ref=dst, send_sem=wsend_sem.at[index], recv_sem=wrecv_sem.at[index],
            device_id=(ty + way[0], tx + way[1]), device_id_type=MESH,
        )

    def ctrl_message(way):
        index = WAYS.index(way)
        return pltpu.make_async_remote_copy(
            src_ref=ctrl_send.at[index], dst_ref=ctrl_recv.at[index],
            send_sem=csend_sem.at[index], recv_sem=crecv_sem.at[index],
            device_id=(ty + way[0], tx + way[1]), device_id_type=MESH,
        )

    def start(make, ways):
        for way in ways:
            @pl.when(inside(way))
            def _(way=way):
                make(way).start()

    def receive(make, ways):
        for way in ways:
            @pl.when(inside(back(way)))
            def _(way=way):
                make(way).wait_recv()

    def sent(make, ways):
        for way in ways:
            @pl.when(inside(way))
            def _(way=way):
                make(way).wait_send()

    def solve_and_send(phase, upward, ready):
        z = (zero,) * 8
        for part in ((2, 1, 0) if upward else (0, 1, 2)):
            z = substitute(phase, part, z, upward)
            if ready is not None:
                ready()
                ready = None
            start(lambda way: message(phase, part, way), WAYS[:2])
            pack_columns(phase, part)
            start(lambda way: message(phase, part, way), WAYS[2:])

    def enter():
        pl.semaphore_wait(barrier, count)
        start(wet_message, WAYS)

    kin[LEVELS] = jnp.zeros((16, 128), F32)

    def factor_body(i, e):
        above, below = list(e), [one, one]
        for step in range(5):
            l = i * 5 + step
            scale = []
            for r in range(2):
                k = kin[l + 1, pl.ds(r, 8, stride=2), :]
                coupled = k * below[r]
                grown = above[r] + coupled
                scale.append(1.0 / grown)
                inva[l, r] = below[r] * scale[r]
                ga[l, r] = coupled * scale[r]
                above[r] = grown + k * above[r]
                below[r] = grown
        return tuple(above[r] * scale[r] for r in range(2))

    lax.fori_loop(
        0, LEVELS // 5, factor_body, tuple(1.0 + kin[0, pl.ds(r, 8, stride=2), :] for r in range(2))
    )

    solve_and_send(0, False, enter)

    for index, way in enumerate(WAYS):
        @pl.when(jnp.logical_not(inside(back(way))))
        def _(index=index, way=way):
            if way in (UP, DOWN):
                target = up_recv if way == UP else down_recv
                def clear(i, _):
                    for phase in range(2):
                        target[phase, i] = zero
                    return 0
                lax.fori_loop(0, LEVELS, clear, 0)
                wrow_recv[index] = zero
            elif way in (RIGHT, LEFT):
                def clear(i, _):
                    for phase in range(2):
                        for c in range(CHUNKS):
                            col_recv[index - 2, phase, c, i] = zero
                    return 0
                lax.fori_loop(0, 8, clear, 0)
                for r in range(2):
                    wcol_recv[index - 2, r] = zero
            else:
                for phase in range(2):
                    for c in range(CHUNKS):
                        corner_recv[index - 4, phase, c] = zero
                wcorner_recv[index - 4] = zero
            ctrl_recv[index] = zero

    for copy in small[1:]:
        copy.wait()

    shift = cols_n.bit_length() - 1
    own_row = (owner[...] >> shift) - ty
    own_col = (owner[...] & (cols_n - 1)) - tx
    cell = ((own_row + 1) * 3 + own_col + 1) * SLOTS + slot[...]
    numbers = lax.broadcasted_iota(jnp.int32, (9 * SLOTS, 128), 0)
    for row in range(16):
        hit = numbers == cell[row:row + 1, :]
        onehot[:, row * 128:(row + 1) * 128] = jnp.where(hit, 1.0, 0.0).astype(jnp.bfloat16)

    def coef_body(j, acc):
        here = quad == j
        return tuple(
            jnp.where(here, coef[v, part * CHUNK + j], acc[part * 4 + v])
            for part in range(CHUNKS) for v in range(4)
        )

    acc = lax.fori_loop(0, CHUNK, coef_body, (zero,) * (4 * CHUNKS))
    for part in range(CHUNKS):
        for v in range(4):
            c_col[part, v] = acc[part * 4 + v]

    source = lax.broadcasted_iota(jnp.int32, (256, 128), 0) & 127
    target = lax.broadcasted_iota(jnp.int32, (256, 128), 1)
    beside_mix[...] = jnp.where(
        (source == target - 1) | (source == target + 1), 1.0, 0.0
    ).astype(jnp.bfloat16)


    mid = (pos == 1) | (pos == 2)
    rim_lanes = (lane < 2) | (lane >= 126)

    def beside_product(levels):
        x = jnp.concatenate([x for level in levels for x in level[:2 * MIXED]], axis=0)
        high = x.astype(jnp.bfloat16)
        both = jnp.concatenate([high, (x - high.astype(F32)).astype(jnp.bfloat16)], axis=1)
        y = jnp.dot(both, beside_mix[...], preferred_element_type=F32)
        return lambda step, n: y[16 * MIXED * step + 8 * n:16 * MIXED * step + 8 * n + 8]

    def neighbour_sums():
        def body(i, _):
            z = [[field[i * UF + step, n] for n in range(8)] for step in range(UF)]
            product = beside_product(z)
            for step in range(UF):
                l = i * UF + step
                for v in range(4):
                    above, below = row_around(z[step][2 * v], z[step][2 * v + 1], 0.0)
                    for r in range(2):
                        n = 2 * v + r
                        if v < MIXED:
                            beside = product(step, n)
                        else:
                            west, east = col_around(z[step][n], 0.0)
                            beside = west + east
                        bulk[l, n] = (above[r] + below[r]) + beside
                        if v == 2:
                            buoy[l, r] = east - west
                        if v == 3:
                            buoy[l, r] = buoy[l, r] + (below[r] - above[r])
            return 0

        lax.fori_loop(0, LEVELS // UF, body, 0)

    def inner_stencil(final):
        def body(i, _):
            d = [
                [
                    w_own[n % 2] * bulk[i * US + step, n] - n_own[n % 2] * field[i * US + step, n]
                    for n in range(8)
                ]
                for step in range(US)
            ]
            product = beside_product(d)
            for step in range(US):
                l = i * US + step
                z = [[field[l, 2 * v + r] for r in range(2)] for v in range(4)]
                for v in range(4):
                    above, below = row_around(d[step][2 * v], d[step][2 * v + 1], 0.0)
                    for r in range(2):
                        n = 2 * v + r
                        if v < MIXED:
                            beside = product(step, n)
                        else:
                            west, east = col_around(d[step][n], 0.0)
                            beside = west + east
                        second = ((above[r] + below[r]) + beside) - n_own[r] * d[step][n]
                        if final:
                            second = second * w_own[r]
                        value = z[v][r] - coef[v, l] * second
                        if v == 0:
                            value = value - (0.25 * THERMAL) * buoy[l, r]
                        elif v == 1:
                            value = value + (0.25 * HALINE) * buoy[l, r]
                        elif v == 2:
                            value = value - CORIOLIS * z[3][r]
                        else:
                            value = value + CORIOLIS * z[2][r]
                        bulk[l, n] = value
            return 0

        lax.fori_loop(0, LEVELS // US, body, 0)

    def outer_stencil(phase, part, carry, final):
        receive(lambda way: message(phase, part, way), WAYS)
        corner = corner_of(*[corner_recv[n, phase, part] for n in range(4)])
        kpack[...] = swap(corner)
        u = [
            [
                jnp.where(
                    pos < 2, col_recv[0, phase, part, 2 * v + r], col_recv[1, phase, part, 2 * v + r]
                )
                for r in range(2)
            ]
            for v in range(4)
        ]
        turned = [[swap(u[v][r]) for r in range(2)] for v in range(4)]
        for v in range(4):
            edge = srl(corner, 7 - 2 * v)
            total = packed_sum(u[v], [col_send[phase, part, 2 * v + r] for r in range(2)], edge)
            added = [jnp.where(mid, wcol_send[r] * turned[v][r], 0.0) for r in range(2)]
            above, below = row_around(added[0], added[1], 0.0)
            for r in range(2):
                outside = swap(w_col[r] * total[r] - n_col[r] * u[v][r])
                second = jnp.where(
                    mid,
                    above[r] + below[r] - n_rim[r] * added[r] + outside,
                    jnp.where(pos == 0, lrl(added[r], -1), lrl(added[r], 1)),
                )
                change = -c_col[part, v] * (wcol_send[r] * second)
                if v < 2:
                    slope = jnp.where(
                        pos == 1, turned[2][r], jnp.where(pos == 2, -turned[2][r], 0.0)
                    )
                    change = change + (-0.25 * THERMAL if v == 0 else 0.25 * HALINE) * slope
                rim[2 * v + r] = change

        def body(i, carry):
            for step in range(UC):
                m = i * UC + step
                j = CHUNK - 1 - m if final else m
                l = part * CHUNK + j
                turn = 126 - 4 * j
                line, beyond = halo_rows(
                    up_recv[phase, l], down_recv[phase, l], up_send[phase, l], down_send[phase, l]
                )
                beside = col_around(line, lrl(kpack[...], turn))
                outside = w_halo[...] * (beyond + beside[0] + beside[1]) - n_halo[...] * line
                added = w_line[...] * line
                beside = col_around(added, 0.0)
                nearest = outside + beside[0] + beside[1] - n_line[...] * added
                gains = jnp.where(
                    pair < 2,
                    jnp.where(pair == 0, coef[0, l], coef[1, l]),
                    jnp.where(pair == 2, coef[2, l], coef[3, l]),
                )
                slope = jnp.where(even, line, -line)
                slope = jnp.where(
                    pair == 0,
                    (-0.25 * THERMAL) * srl(slope, 2),
                    jnp.where(pair == 1, (0.25 * HALINE) * srl(slope, 4), 0.0),
                )
                nearest = slope - gains * (w_line[...] * nearest)
                further = -gains * (w_next[...] * added)
                new = []
                for v in range(4):
                    near = srl(nearest, 7 - 2 * v)
                    far = srl(further, 7 - 2 * v)
                    parts = (
                        jnp.where(top, near, jnp.where(bottom, far, 0.0)),
                        jnp.where(top, far, jnp.where(bottom, near, 0.0)),
                    )
                    for r in range(2):
                        n = 2 * v + r
                        new.append(
                            bulk[l, n] + parts[r] + jnp.where(rim_lanes, lrl(rim[n], turn), 0.0)
                        )
                if final:
                    for n in range(8):
                        outs[l, n // 2, pl.ds(n % 2, 8, stride=2), :] = new[n]
                else:
                    gain, y = carry
                    masked = [new[n] * w_own[n % 2] for n in range(8)]
                    y = tuple(masked[n] + gain[n % 2] * y[n] for n in range(8))
                    for n in range(8):
                        field[l, n] = y[n]
                    if part == 0 and step == 0:
                        @pl.when(i == 0)
                        def _():
                            for n in range(8):
                                surf[n] = surf[n] + masked[n]
                    carry = ((ga[l, 0], ga[l, 1]), y)
            return carry

        return lax.fori_loop(0, CHUNK // UC, body, carry)

    neighbour_sums()

    receive(wet_message, WAYS)
    wk = corner_of(wcorner_recv[0], wcorner_recv[1], wcorner_recv[2], wcorner_recv[3])
    wu2 = [jnp.where(pos < 2, wcol_recv[0, r], wcol_recv[1, r]) for r in range(2)]
    counts = packed_sum(wu2, [wcol_send[r] for r in range(2)], srl(wk, 7))
    for r in range(2):
        w_col[r] = wu2[r]
        n_col[r] = counts[r]
    line, beyond = halo_rows(wrow_recv[0], wrow_recv[1], wrow_send[0], wrow_send[1])
    beside = col_around(line, lrl(swap(wk), 126))
    w_halo[...] = line
    n_halo[...] = beyond + beside[0] + beside[1]
    above, below = row_around(w[0], w[1], srl(line, 7))
    for r in range(2):
        beside = col_around(w[r], lrl(swap(wu2[r]), 126))
        n_own[r] = above[r] + below[r] + beside[0] + beside[1]
    counts = [n_own[r] for r in range(2)]
    for r in range(2):
        n_rim[r] = tile4(counts[r])
    n_up, n_down = row_pack([counts] * 4)
    w_line[...] = jnp.where(even, srl(wd, -1), srl(wu, 1))
    n_line[...] = jnp.where(even, srl(n_down, -1), srl(n_up, 1))
    w_next[...] = jnp.where(even, wd, wu)

    inner_stencil(False)
    carry = ((zero, zero), (zero,) * 8)
    for part in range(CHUNKS):
        carry = outer_stencil(0, part, carry, False)

    solve_and_send(1, True, None)

    for v in range(4):
        for r in range(2):
            surf_rows[v, pl.ds(r, 8, stride=2), :] = surf[v * 2 + r]
    values = jnp.concatenate(
        [jnp.concatenate([surf_rows[:, row, :] for row in range(16)], axis=1)] * 2, axis=0
    )
    high = values.astype(jnp.bfloat16).astype(F32)
    rest = values - high
    middle = rest.astype(jnp.bfloat16).astype(F32)
    low = rest - middle
    pieces = jnp.concatenate([high, middle, low, low], axis=0).astype(jnp.bfloat16)
    sums = lax.dot_general(
        pieces, onehot[...], (((1,), (1,)), ((), ())), preferred_element_type=F32
    )
    sums = (sums[0:8] + sums[8:16] + sums[16:24]) * FLUX_SCALE
    near = sums[:, 0:128]
    for index, way in enumerate(WAYS):
        q = (way[0] + 1) * 3 + way[1] + 1
        if q < 8:
            ctrl_send[index] = lrl(near, -SLOTS * q)
        else:
            ctrl_send[index] = zero
            ctrl_send[index, :, 0:SLOTS] = sums[:, 128:128 + SLOTS]
    start(ctrl_message, WAYS)

    neighbour_sums()
    inner_stencil(True)

    for part in (2, 1, 0):
        outer_stencil(1, part, 0, True)

    receive(ctrl_message, WAYS)
    total = lrl(near, -SLOTS * 4)
    for index in range(8):
        total = total + ctrl_recv[index]
    sens[...] = total[0:4, 0:SLOTS]

    sent(wet_message, WAYS)
    sent(ctrl_message, WAYS)
    for phase in range(2):
        for part in range(CHUNKS):
            sent(lambda way: message(phase, part, way), WAYS)


def build(rows_n, cols_n):
    hbm = pl.BlockSpec(memory_space=pltpu.HBM)
    vmem = pl.BlockSpec(memory_space=pltpu.VMEM)
    tile = (8, 128)
    scratch = [
        pltpu.VMEM((LEVELS, 4, 16, 128), F32),
        pltpu.VMEM((LEVELS + 1, 16, 128), F32),
        pltpu.SMEM((4, LEVELS), F32),
        pltpu.VMEM((16, 128), jnp.int32),
        pltpu.VMEM((16, 128), jnp.int32),
        pltpu.VMEM((16, 128), jnp.int32),
        pltpu.VMEM((LEVELS, 8) + tile, F32),
        pltpu.VMEM((LEVELS, 8) + tile, F32),
        pltpu.VMEM((LEVELS, 2) + tile, F32),
        pltpu.VMEM((LEVELS, 2) + tile, F32),
        pltpu.VMEM((LEVELS, 2) + tile, F32),
        pltpu.VMEM((LEVELS, 2) + tile, F32),
        pltpu.VMEM((LEVELS, 2) + tile, F32),
        pltpu.VMEM((16, 128), F32),
        pltpu.VMEM((2,) + tile, F32),
        pltpu.VMEM((2,) + tile, F32),
        pltpu.VMEM(tile, F32),
        pltpu.VMEM(tile, F32),
        pltpu.VMEM((2,) + tile, F32),
        pltpu.VMEM((2,) + tile, F32),
        pltpu.VMEM((2,) + tile, F32),
        pltpu.VMEM(tile, F32),
        pltpu.VMEM(tile, F32),
        pltpu.VMEM(tile, F32),
        pltpu.VMEM((CHUNKS, 4) + tile, F32),
        pltpu.VMEM((2, LEVELS) + tile, F32),
        pltpu.VMEM((2, LEVELS) + tile, F32),
        pltpu.VMEM((2, CHUNKS, 8) + tile, F32),
        pltpu.VMEM((2, CHUNKS) + tile, F32),
        pltpu.VMEM((2, LEVELS) + tile, F32),
        pltpu.VMEM((2, LEVELS) + tile, F32),
        pltpu.VMEM((2, 2, CHUNKS, 8) + tile, F32),
        pltpu.VMEM((4, 2, CHUNKS) + tile, F32),
        pltpu.VMEM((2,) + tile, F32),
        pltpu.VMEM((2,) + tile, F32),
        pltpu.VMEM(tile, F32),
        pltpu.VMEM((2,) + tile, F32),
        pltpu.VMEM((2, 2) + tile, F32),
        pltpu.VMEM((4,) + tile, F32),
        pltpu.VMEM((8,) + tile, F32),
        pltpu.VMEM(tile, F32),
        pltpu.VMEM((256, 128), jnp.bfloat16),
        pltpu.VMEM((8,) + tile, F32),
        pltpu.VMEM((4, 16, 128), F32),
        pltpu.VMEM((9 * SLOTS, 16 * 128), jnp.bfloat16),
        pltpu.VMEM((8,) + tile, F32),
        pltpu.VMEM((8,) + tile, F32),
        pltpu.SemaphoreType.DMA((2, CHUNKS)),
        pltpu.SemaphoreType.DMA((4,)),
        pltpu.SemaphoreType.DMA((2, CHUNKS, 8)),
        pltpu.SemaphoreType.DMA((2, CHUNKS, 8)),
        pltpu.SemaphoreType.DMA((8,)),
        pltpu.SemaphoreType.DMA((8,)),
        pltpu.SemaphoreType.DMA((8,)),
        pltpu.SemaphoreType.DMA((8,)),
    ]

    def body(*refs):
        kernel(rows_n, cols_n, *refs)

    return pl.pallas_call(
        body,
        out_shape=(pltpu.VMEM((LEVELS, 4, 16, 128), F32), pltpu.VMEM((4, SLOTS), F32)),
        in_specs=[hbm] * 6,
        out_specs=(vmem, vmem),
        scratch_shapes=scratch,
        compiler_params=pltpu.CompilerParams(
            collective_id=0, has_side_effects=True, vmem_limit_bytes=48 << 20
        ),
    )


def write_out(cotangent, sens):
    def body(x, y, x_out, y_out, sem):
        span = LEVELS // OUT_PARTS
        copies = [
            pltpu.make_async_copy(
                x.at[pl.ds(n * span, span)], x_out.at[pl.ds(n * span, span)], sem.at[n]
            )
            for n in range(OUT_PARTS)
        ]
        copies.append(pltpu.make_async_copy(y, y_out, sem.at[OUT_PARTS]))
        for copy in copies:
            copy.start()
        for copy in copies:
            copy.wait()

    place = pl.BlockSpec(memory_space=pl.ANY)
    hbm = pl.BlockSpec(memory_space=pltpu.HBM)
    return pl.pallas_call(
        body,
        out_shape=(
            jax.ShapeDtypeStruct(cotangent.shape, F32), jax.ShapeDtypeStruct(sens.shape, F32),
        ),
        in_specs=[place, place],
        out_specs=(hbm, hbm),
        scratch_shapes=[pltpu.SemaphoreType.DMA((OUT_PARTS + 1,))],
    )(*[pltpu.with_memory_space_constraint(a, pltpu.VMEM) for a in (cotangent, sens)])


def solution(mesh):
    def per_device(cotangent, mixing, coef, *masks):
        call = build(mesh.shape["ty"], mesh.shape["tx"])
        args = (cotangent, mixing, coef.T, *masks)
        return write_out(*call(*[pltpu.with_memory_space_constraint(a, pltpu.HBM) for a in args]))

    return jax.shard_map(
        per_device,
        mesh=mesh,
        in_specs=(
            P(None, None, "ty", "tx"),
            P(None, "ty", "tx"),
            P(),
            P("ty", "tx"),
            P("ty", "tx"),
            P("ty", "tx"),
        ),
        out_specs=(P(None, None, "ty", "tx"), P(None, ("ty", "tx"))),
        check_vma=False,
    )
```
